32 devices in a mesh: dp: 16 (over z, x, core), tensor: 2 (over y).
Axes of the slice: x: 2, y: 2, z: 4, core: 2. Of those that a mesh axis runs over, the one named last changes fastest.
Arguments:
- inputs: float32 [512, 64, 768], P('tensor', 'dp'), may hold values from -6 to 6
- lengths: int32 [64], P('dp'), may hold values from 128 to 512, as said below
- query_weight: bfloat16 [768, 768], P('dp', 'tensor'), may hold values from -0.21875 to 0.21875
- key_weight: bfloat16 [768, 768], P('dp', 'tensor'), may hold values from -0.21875 to 0.21875
- value_weight: bfloat16 [768, 768], P('dp', 'tensor'), may hold values from -0.21875 to 0.21875
- query_bias: float32 [768], replicated, may hold values from -3 to 3
- value_bias: float32 [768], replicated, may hold values from -3 to 3
- out_weight: bfloat16 [768, 768], P('tensor', 'dp'), may hold values from -1.75 to 1.75
- out_bias: float32 [768], replicated, may hold values from -3 to 3
- first_gain: float32 [768], replicated, may hold values from 0.25 to 1.75
- first_shift: float32 [768], replicated, may hold values from -2 to 2
- input_projection_weight: bfloat16 [768, 3072], P('dp', 'tensor'), may hold values from -0.21875 to 0.21875
- input_projection_bias: float32 [3072], replicated, may hold values from -3 to 3
- output_projection_weight: bfloat16 [3072, 768], P('tensor', 'dp'), may hold values from -0.109375 to 0.109375
- output_projection_bias: float32 [768], replicated, may hold values from -3 to 3
- second_gain: float32 [768], replicated, may hold values from 0.25 to 1.75
- second_shift: float32 [768], replicated, may hold values from -2 to 2
- out_cotangent: float32 [512, 64, 768], P('tensor', 'dp'), may hold values from -6 to 6
Outputs:
- outputs: float32 [512, 64, 768], P('tensor', 'dp')
- input_grad: float32 [512, 64, 768], P('tensor', 'dp')
- query_weight_grad: float32 [768, 768], P('dp', 'tensor')
- key_weight_grad: float32 [768, 768], P('dp', 'tensor')
- value_weight_grad: float32 [768, 768], P('dp', 'tensor')
- query_bias_grad: float32 [768], replicated
- value_bias_grad: float32 [768], replicated
- out_weight_grad: float32 [768, 768], P('tensor', 'dp')
- out_bias_grad: float32 [768], replicated
- first_gain_grad: float32 [768], replicated
- first_shift_grad: float32 [768], replicated
- up_weight_grad: float32 [768, 3072], P('dp', 'tensor')
- up_bias_grad: float32 [3072], replicated
- down_weight_grad: float32 [3072, 768], P('tensor', 'dp')
- down_bias_grad: float32 [768], replicated
- second_gain_grad: float32 [768], replicated
- second_shift_grad: float32 [768], replicated
The draws below stay inside these ranges and needn't reach their ends.
Inputs may be any that keep to these rules, and one draw needn't show every extreme that they name: `lengths`: valid positions of each sequence. In every aligned block of 4 sequences one, at a drawn place, has more than 448 valid positions; one sequence of all, at a drawn place, has exactly 512.
All inputs are finite; a program needn't handle non-finite values.
Results may differ from the reference program's by a relative error of at most 0.017.
Values may be sent and summed in bfloat16 or wider, within the bound.
No kernel may reach another device: no remote copies, remote signals or barrier semaphores. Data moves between devices by JAX's collectives and lax.ppermute only.
A program may use at most 192 MiB of HBM per device.

```python
import jax
import jax.numpy as jnp
from jax import lax

D = 768
H = 12
HD = 64
FF = 3072
SEQ = 512
SEQ_DEV = 4
SEQS = 64


def draw_lengths(key, part):
    key = jax.random.fold_in(key, 7)
    key_lengths, key_chosen, key_long, key_full = jax.random.split(key, 4)
    drawn = jax.random.randint(key_lengths, (SEQS,), SEQ // 4, SEQ + 1)
    chosen = jax.random.randint(key_chosen, (SEQS // SEQ_DEV,), 0, SEQ_DEV)
    long_draw = jax.random.randint(key_long, (SEQS // SEQ_DEV, SEQ_DEV), SEQ - SEQ // 8 + 1, SEQ + 1).reshape(SEQS)
    long_mask = (jnp.arange(SEQ_DEV)[None, :] == chosen[:, None]).reshape(SEQS)
    full_place = jax.random.randint(key_full, (), 0, SEQS)
    result = jnp.where(long_mask, long_draw, drawn)
    result = jnp.where(jnp.arange(SEQS) == full_place, SEQ, result)
    return result.astype(jnp.int32)


def shard_levels(stream_key, dims, shards, low, largest):
    level = 1.0
    for position, parts in shards:
        draws = jax.random.uniform(jax.random.fold_in(jax.random.fold_in(stream_key, 6), position), (parts,), jnp.float32, low / len(shards), largest / len(shards))
        level = level * jnp.repeat(jnp.exp(draws), dims[position] // parts).reshape((-1,) + (1,) * (len(dims) - 1 - position))
    return level


def gaussian(rng, dims, deviation, reach, cuts=(), kind=jnp.bfloat16):
    level = shard_levels(rng, dims, cuts, -0.22, 0.18) if cuts else 1.0
    entries = jax.random.normal(rng, dims, jnp.float32) * deviation * level
    return jnp.minimum(jnp.maximum(entries, -reach), reach).astype(kind)


def setup_inputs(seed: int = 0) -> dict:
    streams_of = jax.random.split(jax.random.key(seed), 19)
    return {
        "inputs": gaussian(streams_of[0], (SEQ, SEQS, D), 1.0, 6.0, ((0, 2), (1, 16)), jnp.float32),
        "lengths": draw_lengths(jax.random.fold_in(streams_of[18], 71), 0),
        "query_weight": gaussian(streams_of[2], (D, D), D ** -0.5, 0.21875, ((0, 16), (1, 2))),
        "key_weight": gaussian(streams_of[3], (D, D), D ** -0.5, 0.21875, ((0, 16), (1, 2))),
        "value_weight": gaussian(streams_of[4], (D, D), D ** -0.5, 0.21875, ((0, 16), (1, 2))),
        "query_bias": gaussian(streams_of[5], (D,), 0.5, 3.0, (), jnp.float32),
        "value_bias": gaussian(streams_of[6], (D,), 0.5, 3.0, (), jnp.float32),
        "out_weight": gaussian(streams_of[7], (D, D), (D * 8 // SEQ) ** -0.5, 1.75, ((0, 2), (1, 16))),
        "out_bias": gaussian(streams_of[8], (D,), 0.5, 3.0, (), jnp.float32),
        "first_gain": jnp.clip(1.0 + 0.15 * jax.random.normal(streams_of[9], (D,), jnp.float32), 0.25, 1.75),
        "first_shift": gaussian(streams_of[10], (D,), 0.3, 2.0, (), jnp.float32),
        "input_projection_weight": gaussian(streams_of[11], (D, FF), D ** -0.5, 0.21875, ((0, 16), (1, 2))),
        "input_projection_bias": gaussian(streams_of[12], (FF,), 0.5, 3.0, (), jnp.float32),
        "output_projection_weight": gaussian(streams_of[13], (FF, D), FF ** -0.5, 0.109375, ((0, 2), (1, 16))),
        "output_projection_bias": gaussian(streams_of[14], (D,), 0.5, 3.0, (), jnp.float32),
        "second_gain": jnp.clip(1.0 + 0.15 * jax.random.normal(streams_of[15], (D,), jnp.float32), 0.25, 1.75),
        "second_shift": gaussian(streams_of[16], (D,), 0.3, 2.0, (), jnp.float32),
        "out_cotangent": gaussian(streams_of[17], (SEQ, SEQS, D), 1.0, 6.0, ((0, 2), (1, 16)), jnp.float32),
    }


@jax.custom_vjp
def low(v):
    return lax.optimization_barrier(v.astype(jnp.bfloat16)).astype(jnp.float32)

@jax.custom_vjp
def low_back(v):
    return v

def low_keep(v):
    return (low(v), None)

def low_pass(kept, grad):
    return (grad,)

def back_keep(v):
    return (v, None)

def back_low(kept, grad):
    return (low(grad),)
low.defvjp(low_keep, low_pass)
low_back.defvjp(back_keep, back_low)
NORM_EPSILON = 1e-12

def matrix_product(form, left, right):
    return jnp.einsum(form, left, right, precision=lax.Precision.HIGHEST)

def layer_norm(resid, gain_vec, shift_vec):
    mean_value = lax.optimization_barrier(jnp.mean(resid, -1, keepdims=True))
    centred = resid - mean_value
    variance = lax.optimization_barrier(jnp.mean(centred * centred, -1, keepdims=True))
    return centred * lax.rsqrt(variance + NORM_EPSILON) * gain_vec + shift_vec

def encoder_block(block_row_span, seq_lengths, weights):
    query_weight, key_weight, value_weight, query_bias, value_bias, out_weight, out_bias, first_gain, first_shift, input_projection_weight, input_projection_bias, output_projection_weight, output_projection_bias, second_gain, second_shift = weights
    length = block_row_span.shape[0]
    batch_size = block_row_span.shape[1]
    head_shape = (batch_size, length, H, HD)
    rows_low = low(block_row_span)
    queries = low(low_back(matrix_product('lsd,dc->slc', rows_low, query_weight) + query_bias))
    keys_low = low(low_back(matrix_product('lsd,dc->slc', rows_low, key_weight)))
    values_low = low(low_back(matrix_product('lsd,dc->slc', rows_low, value_weight) + value_bias))
    scores = low_back(matrix_product('sqhd,skhd->shqk', queries.reshape(head_shape), keys_low.reshape(head_shape)) * HD ** (-0.5))
    key_valid = jnp.arange(length, dtype=jnp.int32)[None, :] < seq_lengths[:, None]
    scores = jnp.where(key_valid[:, None, None, :], scores, -1e+30)
    soft_weights = low(jax.nn.softmax(scores, axis=-1))
    context = matrix_product('shqk,skhd->sqhd', soft_weights, values_low.reshape(head_shape)).reshape(batch_size, length, H * HD)
    context = low(low_back(context))
    attention = low_back(matrix_product('slc,cd->lsd', context, out_weight)) + out_bias
    hidden = layer_norm(block_row_span + attention, first_gain, first_shift)
    hidden_reduced_precision = low(hidden)
    hidden_preactivation = low_back(matrix_product('zhx,xm->zhm', hidden_reduced_precision, input_projection_weight) + input_projection_bias)
    hidden_activation = low(jax.nn.gelu(hidden_preactivation, approximate=False))
    feedforward_branch = low_back(matrix_product('kng,gw->knw', hidden_activation, output_projection_weight)) + output_projection_bias
    return layer_norm(hidden + feedforward_branch, second_gain, second_shift)

def reference(inputs, lengths, query_weight, key_weight, value_weight, query_bias, value_bias, out_weight, out_bias, first_gain, first_shift, input_projection_weight, input_projection_bias, output_projection_weight, output_projection_bias, second_gain, second_shift, out_cotangent):
    blocks = SEQS // SEQ_DEV

    def forward(rows_in, *weights):
        stacked = rows_in.reshape(SEQ, blocks, SEQ_DEV, D).transpose(1, 0, 2, 3)
        grouped = lengths.reshape(blocks, SEQ_DEV)

        def one_block(packed):
            return encoder_block(packed[0], packed[1], weights)
        result = lax.map(jax.checkpoint(one_block), (stacked, grouped))
        return result.transpose(1, 0, 2, 3).reshape(SEQ, SEQS, D)
    params = (query_weight, key_weight, value_weight, query_bias, value_bias, out_weight, out_bias, first_gain, first_shift, input_projection_weight, input_projection_bias, output_projection_weight, output_projection_bias, second_gain, second_shift)
    floats = [tensor_in.astype(jnp.float32) for tensor_in in params]
    outputs, pullback = jax.vjp(forward, inputs.astype(jnp.float32), *floats)
    gradients = pullback(out_cotangent.astype(jnp.float32))
    return (outputs, gradients[0], gradients[1], gradients[2], gradients[3], gradients[4], gradients[5], gradients[6], gradients[7], gradients[8], gradients[9], gradients[10], gradients[11], gradients[12], gradients[13], gradients[14], gradients[15])
```

```python
import functools

import jax
import jax.numpy as jnp
from jax import lax
from jax.experimental import pallas as pl
from jax.experimental.pallas import tpu as pltpu
from jax.sharding import PartitionSpec as P

D = 768
H = 12
HD = 64
FF = 3072

NORM_EPSILON = 1e-12
BF = jnp.bfloat16
F32 = jnp.float32


def dot(a, b, da, db):
    return lax.dot_general(a, b, (((da,), (db,)), ((), ())), preferred_element_type=F32)


def layer_norm(resid, gain_vec, shift_vec):
    mean_value = jnp.mean(resid, -1, keepdims=True)
    centred = resid - mean_value
    variance = jnp.mean(centred * centred, -1, keepdims=True)
    inv_std = lax.rsqrt(variance + NORM_EPSILON)
    normed = centred * inv_std
    return (normed * gain_vec + shift_vec, normed, inv_std)


def norm_back(grad_in, normed, inv_std, gain_vec):
    scaled = grad_in * gain_vec
    return inv_std * (
        scaled
        - jnp.mean(scaled, -1, keepdims=True)
        - normed * jnp.mean(scaled * normed, -1, keepdims=True)
    )


def gelu_both(v):
    z = jnp.abs(v) * (0.5**0.5)
    t = 1.0 / (1.0 + 0.3275911 * z)
    gauss = jnp.exp(-0.5 * v * v)
    poly = t * (
        0.5 * 0.254829592
        + t * (0.5 * -0.284496736 + t * (0.5 * 1.421413741 + t * (0.5 * -1.453152027 + t * (0.5 * 1.061405429))))
    )
    tail = poly * gauss
    phi_cum = jnp.where(v < 0, tail, 1.0 - tail)
    return v * phi_cum, phi_cum + v * gauss * 0.3989422804014327


def attend_forward_kernel(heads, half, lens, tindex, q_ref, k_ref, v_ref, ko_ref, vo_ref, ctx_ref, lse_ref):
    seq = pl.program_id(1)
    length = lens[seq]
    own = tindex[0] * half
    other = (1 - tindex[0]) * half
    lane = lax.broadcasted_iota(jnp.int32, (1, half), 1)
    bias_own = jnp.where(lane + own < length, 0.0, -1e30)
    bias_oth = jnp.where(lane + other < length, 0.0, -1e30)
    col = lax.broadcasted_iota(jnp.int32, (half, 128), 1)
    lse_tile = jnp.zeros((half, 128), F32)
    for h in range(heads):
        sl = slice(h * HD, (h + 1) * HD)
        q = q_ref[0, :, sl]
        s_own = dot(q, k_ref[0, :, sl], 1, 1) + bias_own
        s_oth = dot(q, ko_ref[0, :, sl], 1, 1) + bias_oth
        m = jnp.maximum(jnp.max(s_own, -1, keepdims=True), jnp.max(s_oth, -1, keepdims=True))
        e_own = jnp.exp(s_own - m)
        e_oth = jnp.exp(s_oth - m)
        total = jnp.sum(e_own, -1, keepdims=True) + jnp.sum(e_oth, -1, keepdims=True)
        c = dot(e_own.astype(BF), v_ref[0, :, sl], 1, 0) + dot(e_oth.astype(BF), vo_ref[0, :, sl], 1, 0)
        ctx_ref[:, sl] = (c / total).astype(BF)
        lse_tile = jnp.where(col == h, m + jnp.log(total), lse_tile)
    lse_ref[0] = lse_tile


def attend_backward_kernel(
    heads, half, lens, tindex, q_ref, k_ref, v_ref, ko_ref, vo_ref, ctx_ref, lse_ref, dctx_ref, own_ref, oth_ref
):
    seq = pl.program_id(1)
    width = heads * HD
    length = lens[seq]
    own = tindex[0] * half
    other = (1 - tindex[0]) * half
    row = lax.broadcasted_iota(jnp.int32, (half, 1), 0)
    bias_own = jnp.where(row + own < length, 0.0, -1e30)
    bias_oth = jnp.where(row + other < length, 0.0, -1e30)
    lse_rows = jnp.transpose(lse_ref[0])
    prod = ctx_ref[...].astype(F32) * dctx_ref[...].astype(F32)
    col = lax.broadcasted_iota(jnp.int32, (half, 128), 1)
    delta_tile = jnp.zeros((half, 128), F32)
    for h in range(heads):
        delta_tile = jnp.where(
            col == h, jnp.sum(prod[:, h * HD : (h + 1) * HD], -1, keepdims=True), delta_tile
        )
    delta_rows = jnp.transpose(delta_tile)
    for h in range(heads):
        sl = slice(h * HD, (h + 1) * HD)
        q = q_ref[0, :, sl]
        dc = dctx_ref[:, sl]
        lse = lse_rows[h : h + 1, :]
        delta = delta_rows[h : h + 1, :]
        dq = None
        for k_src, v_src, bias, out, base in (
            (k_ref, v_ref, bias_own, own_ref, width),
            (ko_ref, vo_ref, bias_oth, oth_ref, 0),
        ):
            k = k_src[0, :, sl]
            p = jnp.exp(dot(k, q, 1, 1) + bias - lse)
            dp = dot(v_src[0, :, sl], dc, 1, 1)
            ds = (p * (dp - delta)).astype(BF)
            out[0, :, base + h * HD : base + (h + 1) * HD] = dot(ds, q, 1, 0).astype(BF)
            out[0, :, base + width + h * HD : base + width + (h + 1) * HD] = dot(
                p.astype(BF), dc, 1, 0
            ).astype(BF)
            part = dot(ds, k, 0, 0)
            dq = part if dq is None else dq + part
        own_ref[0, :, sl] = (dq * HD**-0.5).astype(BF)


def attend_forward(lengths, tindex, qkv_own, kv_oth, seqs, half):
    halves, rows, width3 = qkv_own.shape
    width = width3 // 3
    heads = width // HD
    spec = lambda j: pl.BlockSpec((1, half, width), lambda t, s, *_: (t, s, j))
    return pl.pallas_call(
        functools.partial(attend_forward_kernel, heads, half),
        grid_spec=pltpu.PrefetchScalarGridSpec(
            num_scalar_prefetch=2,
            grid=(halves, seqs),
            in_specs=[spec(0), spec(1), spec(2), spec(0), spec(1)],
            out_specs=[
                pl.BlockSpec((half, width), lambda t, s, *_: (s, t)),
                pl.BlockSpec((1, half, 128), lambda t, s, *_: (t * seqs + s, 0, 0)),
            ],
        ),
        out_shape=[
            jax.ShapeDtypeStruct((rows, halves * width), BF),
            jax.ShapeDtypeStruct((halves * seqs, half, 128), F32),
        ],
        compiler_params=pltpu.CompilerParams(vmem_limit_bytes=32 * 1024 * 1024),
        cost_estimate=pl.CostEstimate(flops=6_000_000_000, bytes_accessed=9_000_000, transcendentals=7_000_000),
        name="attend_forward",
    )(lengths, tindex, qkv_own, qkv_own, qkv_own, kv_oth, kv_oth)


def attend_backward(lengths, tindex, qkv_own, kv_oth, ctx, lse, dctx, seqs, half):
    halves, rows, width3 = qkv_own.shape
    width = width3 // 3
    heads = width // HD
    spec = lambda j: pl.BlockSpec((1, half, width), lambda t, s, *_: (t, s, j))
    flat = pl.BlockSpec((half, width), lambda t, s, *_: (s, t))
    return pl.pallas_call(
        functools.partial(attend_backward_kernel, heads, half),
        grid_spec=pltpu.PrefetchScalarGridSpec(
            num_scalar_prefetch=2,
            grid=(halves, seqs),
            in_specs=[
                spec(0),
                spec(1),
                spec(2),
                spec(0),
                spec(1),
                flat,
                pl.BlockSpec((1, half, 128), lambda t, s, *_: (t * seqs + s, 0, 0)),
                flat,
            ],
            out_specs=[
                pl.BlockSpec((1, half, 3 * width), lambda t, s, *_: (t, s, 0)),
                pl.BlockSpec((1, half, 2 * width), lambda t, s, *_: (t, s, 0)),
            ],
        ),
        out_shape=[
            jax.ShapeDtypeStruct((halves, rows, 3 * width), BF),
            jax.ShapeDtypeStruct((halves, rows, 2 * width), BF),
        ],
        compiler_params=pltpu.CompilerParams(vmem_limit_bytes=40 * 1024 * 1024),
        cost_estimate=pl.CostEstimate(flops=15_000_000_000, bytes_accessed=20_000_000, transcendentals=7_000_000),
        name="attend_backward",
    )(lengths, tindex, qkv_own, qkv_own, qkv_own, kv_oth, kv_oth, ctx, lse, dctx)


def sum_everywhere(vec, dp_size):
    vec = vec + lax.ppermute(vec, "tensor", [(0, 1), (1, 0)])
    bit = 1
    while bit < dp_size:
        vec = vec + lax.ppermute(vec, "dp", [(i, i ^ bit) for i in range(dp_size)])
        bit *= 2
    return vec


def split_vec(vec, sizes):
    out, at = [], 0
    for size in sizes:
        out.append(lax.slice_in_dim(vec, at, at + size))
        at += size
    return out


def shards(
    inputs,
    lengths,
    query_weight,
    key_weight,
    value_weight,
    query_bias,
    value_bias,
    out_weight,
    out_bias,
    first_gain,
    first_shift,
    input_projection_weight,
    input_projection_bias,
    output_projection_weight,
    output_projection_bias,
    second_gain,
    second_shift,
    out_cotangent,
):
    tensor_index = lax.axis_index("tensor")
    dp_size = lax.axis_size("dp")
    half, seqs, _ = inputs.shape
    rows = half * seqs
    width = D // 2
    hidden_width = FF // 2
    tindex = jnp.reshape(tensor_index, (1,)).astype(jnp.int32)
    everywhere = ("tensor", "dp")

    def gather(packed):
        full = lax.all_gather(packed, everywhere, axis=0, tiled=True)
        return full.reshape(2, D, packed.shape[1])

    def swap(v):
        return lax.ppermute(v, "tensor", [(0, 1), (1, 0)])

    qkv_w = gather(jnp.concatenate([query_weight, key_weight, value_weight], 1))
    out_w = gather(out_weight.T)
    up_w = gather(input_projection_weight)
    down_w = gather(output_projection_weight.T)

    inputs_seq = inputs.transpose(1, 0, 2).reshape(rows, D)
    rows_low = inputs_seq.astype(BF)
    rows_other = swap(rows_low)
    zeros = jnp.zeros((width,), F32)
    own_parts, oth_parts = [], []
    for t in range(2):
        qb = query_bias[t * width : (t + 1) * width]
        vb = value_bias[t * width : (t + 1) * width]
        product = dot(rows_low, qkv_w[t], 1, 0) + jnp.concatenate([qb, zeros, vb])
        scale = jnp.concatenate([jnp.full((width,), HD**-0.5, BF), jnp.ones((2 * width,), BF)])
        own_parts.append(product.astype(BF) * scale)
        product = dot(rows_other, qkv_w[t][:, width:], 1, 0) + jnp.concatenate([zeros, vb])
        oth_parts.append(product.astype(BF))
    qkv_own = jnp.stack(own_parts)
    kv_oth = jnp.stack(oth_parts)
    context, log_sums = attend_forward(lengths, tindex, qkv_own, kv_oth, seqs, half)
    attention = dot(context[:, :width], out_w[0], 1, 1) + dot(context[:, width:], out_w[1], 1, 1)
    hidden, normed_one, inv_one = layer_norm(inputs_seq + attention + out_bias, first_gain, first_shift)
    hidden_low = hidden.astype(BF)
    acts, slopes = [], []
    for t in range(2):
        pre = dot(hidden_low, up_w[t], 1, 0) + input_projection_bias[t * hidden_width : (t + 1) * hidden_width]
        act, slope = gelu_both(pre)
        acts.append(act.astype(BF))
        slopes.append(slope.astype(BF))
    branch = dot(acts[0], down_w[0], 1, 1) + dot(acts[1], down_w[1], 1, 1)
    outputs, normed_two, inv_two = layer_norm(
        hidden + branch + output_projection_bias, second_gain, second_shift
    )
    cotangent = out_cotangent.transpose(1, 0, 2).reshape(rows, D)
    second_grad = norm_back(cotangent, normed_two, inv_two, second_gain)
    second_gain_part = jnp.sum(cotangent * normed_two, axis=0)
    second_shift_part = jnp.sum(cotangent, axis=0)
    down_bias_part = jnp.sum(second_grad, axis=0)
    second_low = second_grad.astype(BF)
    pre_grads, up_bias_parts = [], []
    for t in range(2):
        pre_grad = (dot(second_low, down_w[t], 1, 0) * slopes[t].astype(F32)).astype(BF)
        pre_grads.append(pre_grad)
        up_bias_parts.append(jnp.sum(pre_grad, axis=0, dtype=F32))

    def scatter(parts):
        full = jnp.concatenate([p.astype(BF) for p in parts], 0)
        return lax.psum_scatter(full, everywhere, scatter_dimension=0, tiled=True)

    down_sum = scatter([dot(second_low, acts[t], 0, 0) for t in range(2)])
    up_sum = scatter([dot(hidden_low, pre_grads[t], 0, 0) for t in range(2)])
    hidden_grad = second_grad + (dot(pre_grads[0], up_w[0], 1, 1) + dot(pre_grads[1], up_w[1], 1, 1))
    first_grad = norm_back(hidden_grad, normed_one, inv_one, first_gain)
    first_gain_part = jnp.sum(hidden_grad * normed_one, axis=0)
    first_shift_part = jnp.sum(hidden_grad, axis=0)
    out_bias_part = jnp.sum(first_grad, axis=0)
    first_low = first_grad.astype(BF)
    early = sum_everywhere(
        jnp.concatenate(
            [
                out_bias_part,
                first_gain_part,
                first_shift_part,
                down_bias_part,
                second_gain_part,
                second_shift_part,
                *up_bias_parts,
            ]
        ),
        dp_size,
    )
    out_bias_sum, first_gain_sum, first_shift_sum, down_bias_sum, second_gain_sum, second_shift_sum, up_bias_sum = (
        split_vec(early, [D] * 6 + [FF])
    )
    context_grad = jnp.concatenate([dot(first_low, out_w[t], 1, 0).astype(BF) for t in range(2)], 1)
    out_grads = [dot(first_low, context[:, t * width : (t + 1) * width], 0, 0) for t in range(2)]
    own_grad, oth_grad = attend_backward(
        lengths, tindex, qkv_own, kv_oth, context, log_sums, context_grad, seqs, half
    )
    other_total = dot(oth_grad[0], qkv_w[0][:, width:], 1, 1) + dot(oth_grad[1], qkv_w[1][:, width:], 1, 1)
    from_other = swap(other_total.astype(BF))
    own_total = dot(own_grad[0], qkv_w[0], 1, 1) + dot(own_grad[1], qkv_w[1], 1, 1)
    input_grad = first_grad + (own_total + from_other.astype(F32))
    grads = []
    for t in range(2):
        query_part = dot(rows_low, own_grad[t][:, :width], 0, 0)
        key_value_part = dot(rows_low, own_grad[t][:, width:], 0, 0) + dot(rows_other, oth_grad[t], 0, 0)
        grads.append(jnp.concatenate([query_part.astype(BF), key_value_part.astype(BF), out_grads[t].astype(BF)], 1))
    qkvo_sum = scatter(grads)
    late = sum_everywhere(
        jnp.concatenate(
            [jnp.sum(own_grad[t][:, :width], axis=0, dtype=F32) for t in range(2)]
            + [
                jnp.sum(own_grad[t][:, 2 * width :], axis=0, dtype=F32)
                + jnp.sum(oth_grad[t][:, width:], axis=0, dtype=F32)
                for t in range(2)
            ]
        ),
        dp_size,
    )
    query_bias_sum, value_bias_sum = split_vec(late, [D, D])
    qkvo_sum = qkvo_sum.astype(F32)

    def positions_first(v):
        return v.reshape(seqs, half, D).transpose(1, 0, 2)

    return (
        positions_first(outputs),
        positions_first(input_grad),
        qkvo_sum[:, :width],
        qkvo_sum[:, width : 2 * width],
        qkvo_sum[:, 2 * width : 3 * width],
        query_bias_sum,
        value_bias_sum,
        qkvo_sum[:, 3 * width :].T,
        out_bias_sum,
        first_gain_sum,
        first_shift_sum,
        up_sum.astype(F32),
        up_bias_sum,
        down_sum.astype(F32).T,
        down_bias_sum,
        second_gain_sum,
        second_shift_sum,
    )


def solution(mesh):
    in_specs = (
        P("tensor", "dp", None),
        P("dp"),
        P("dp", "tensor"),
        P("dp", "tensor"),
        P("dp", "tensor"),
        P(),
        P(),
        P("tensor", "dp"),
        P(),
        P(),
        P(),
        P("dp", "tensor"),
        P(),
        P("tensor", "dp"),
        P(),
        P(),
        P(),
        P("tensor", "dp", None),
    )
    out_specs = (
        P("tensor", "dp", None),
        P("tensor", "dp", None),
        P("dp", "tensor"),
        P("dp", "tensor"),
        P("dp", "tensor"),
        P(),
        P(),
        P("tensor", "dp"),
        P(),
        P(),
        P(),
        P("dp", "tensor"),
        P(),
        P("tensor", "dp"),
        P(),
        P(),
        P(),
    )
    return jax.shard_map(shards, mesh=mesh, in_specs=in_specs, out_specs=out_specs, check_vma=False)
```

```python
import functools

import jax
import jax.numpy as jnp
from jax import lax
from jax.experimental import pallas as pl
from jax.experimental.pallas import tpu as pltpu
from jax.sharding import PartitionSpec as P

D = 768
H = 12
HD = 64
FF = 3072

NORM_EPSILON = 1e-12
BF = jnp.bfloat16
F32 = jnp.float32


def dot(a, b, da, db):
    return lax.dot_general(a, b, (((da,), (db,)), ((), ())), preferred_element_type=F32)


def layer_norm(resid, gain_vec, shift_vec):
    mean_value = jnp.mean(resid, -1, keepdims=True)
    centred = resid - mean_value
    variance = jnp.mean(centred * centred, -1, keepdims=True)
    inv_std = lax.rsqrt(variance + NORM_EPSILON)
    normed = centred * inv_std
    return (normed * gain_vec + shift_vec, normed, inv_std)


def norm_back(grad_in, normed, inv_std, gain_vec):
    scaled = grad_in * gain_vec
    return inv_std * (
        scaled
        - jnp.mean(scaled, -1, keepdims=True)
        - normed * jnp.mean(scaled * normed, -1, keepdims=True)
    )


def gelu_both(v):
    z = jnp.abs(v) * (0.5**0.5)
    t = 1.0 / (1.0 + 0.3275911 * z)
    gauss = jnp.exp(-0.5 * v * v)
    poly = t * (
        0.5 * 0.254829592
        + t * (0.5 * -0.284496736 + t * (0.5 * 1.421413741 + t * (0.5 * -1.453152027 + t * (0.5 * 1.061405429))))
    )
    tail = poly * gauss
    phi_cum = jnp.where(v < 0, tail, 1.0 - tail)
    return v * phi_cum, phi_cum + v * gauss * 0.3989422804014327


def attend_forward_kernel(heads, half, lens, tindex, q_ref, k_ref, v_ref, ctx_ref, lse_ref):
    length = lens[pl.program_id(0)]
    lane = lax.broadcasted_iota(jnp.int32, (1, half), 1)
    bias = [jnp.where(lane + place * half < length, 0.0, -1e30) for place in (tindex[0], 1 - tindex[0])]
    col = lax.broadcasted_iota(jnp.int32, (half, 128), 1)
    lse_tile = jnp.zeros((half, 128), F32)
    for h in range(heads):
        sl = slice(h * HD, (h + 1) * HD)
        q = q_ref[:, sl]
        s_own = dot(q, k_ref[0, :, sl], 1, 1) + bias[0]
        s_oth = dot(q, k_ref[1, :, sl], 1, 1) + bias[1]
        m = jnp.maximum(jnp.max(s_own, -1, keepdims=True), jnp.max(s_oth, -1, keepdims=True))
        e_own = jnp.exp(s_own - m)
        e_oth = jnp.exp(s_oth - m)
        total = jnp.sum(e_own, -1, keepdims=True) + jnp.sum(e_oth, -1, keepdims=True)
        c = dot(e_own.astype(BF), v_ref[0, :, sl], 1, 0) + dot(e_oth.astype(BF), v_ref[1, :, sl], 1, 0)
        ctx_ref[:, sl] = (c / total).astype(BF)
        lse_tile = jnp.where(col == h, m + jnp.log(total), lse_tile)
    lse_ref[0] = lse_tile


def attend_backward_kernel(
    heads, half, lens, tindex, q_ref, k_ref, v_ref, ctx_ref, lse_ref, dctx_ref, dq_ref, dk_ref, dv_ref
):
    length = lens[pl.program_id(0)]
    row = lax.broadcasted_iota(jnp.int32, (half, 1), 0)
    bias = [jnp.where(row + place * half < length, 0.0, -1e30) for place in (tindex[0], 1 - tindex[0])]
    lse_rows = jnp.transpose(lse_ref[0])
    prod = ctx_ref[...].astype(F32) * dctx_ref[...].astype(F32)
    col = lax.broadcasted_iota(jnp.int32, (half, 128), 1)
    delta_tile = jnp.zeros((half, 128), F32)
    for h in range(heads):
        delta_tile = jnp.where(
            col == h, jnp.sum(prod[:, h * HD : (h + 1) * HD], -1, keepdims=True), delta_tile
        )
    delta_rows = jnp.transpose(delta_tile)
    for h in range(heads):
        sl = slice(h * HD, (h + 1) * HD)
        q = q_ref[:, sl]
        dc = dctx_ref[:, sl]
        lse = lse_rows[h : h + 1, :]
        delta = delta_rows[h : h + 1, :]
        dq = None
        for i in range(2):
            k = k_ref[i, :, sl]
            p = jnp.exp(dot(k, q, 1, 1) + bias[i] - lse)
            dp = dot(v_ref[i, :, sl], dc, 1, 1)
            ds = (p * (dp - delta)).astype(BF)
            dk_ref[i, :, sl] = dot(ds, q, 1, 0).astype(BF)
            dv_ref[i, :, sl] = dot(p.astype(BF), dc, 1, 0).astype(BF)
            part = dot(ds, k, 0, 0)
            dq = part if dq is None else dq + part
        dq_ref[:, sl] = (dq * HD**-0.5).astype(BF)


def attend_specs(half, width):
    rows = pl.BlockSpec((half, width), lambda s, *_: (s, 0))
    pair = pl.BlockSpec((2, half, width), lambda s, *_: (0, s, 0))
    stat = pl.BlockSpec((1, half, 128), lambda s, *_: (s, 0, 0))
    return rows, pair, stat


def attend_forward(lengths, tindex, q, k, v, seqs):
    rows, width = q.shape
    half = rows // seqs
    flat, pair, stat = attend_specs(half, width)
    return pl.pallas_call(
        functools.partial(attend_forward_kernel, width // HD, half),
        grid_spec=pltpu.PrefetchScalarGridSpec(
            num_scalar_prefetch=2, grid=(seqs,), in_specs=[flat, pair, pair], out_specs=[flat, stat]
        ),
        out_shape=[
            jax.ShapeDtypeStruct((rows, width), BF),
            jax.ShapeDtypeStruct((seqs, half, 128), F32),
        ],
        compiler_params=pltpu.CompilerParams(vmem_limit_bytes=24 * 1024 * 1024),
        cost_estimate=pl.CostEstimate(flops=8_000_000_000, bytes_accessed=5_000_000, transcendentals=3_500_000),
        name="attend_forward",
    )(lengths, tindex, q, k, v)


def attend_backward(lengths, tindex, q, k, v, ctx, lse, dctx, seqs):
    rows, width = q.shape
    half = rows // seqs
    flat, pair, stat = attend_specs(half, width)
    return pl.pallas_call(
        functools.partial(attend_backward_kernel, width // HD, half),
        grid_spec=pltpu.PrefetchScalarGridSpec(
            num_scalar_prefetch=2,
            grid=(seqs,),
            in_specs=[flat, pair, pair, flat, stat, flat],
            out_specs=[flat, pair, pair],
        ),
        out_shape=[
            jax.ShapeDtypeStruct((rows, width), BF),
            jax.ShapeDtypeStruct((2, rows, width), BF),
            jax.ShapeDtypeStruct((2, rows, width), BF),
        ],
        compiler_params=pltpu.CompilerParams(vmem_limit_bytes=24 * 1024 * 1024),
        cost_estimate=pl.CostEstimate(flops=16_000_000_000, bytes_accessed=10_000_000, transcendentals=3_500_000),
        name="attend_backward",
    )(lengths, tindex, q, k, v, ctx, lse, dctx)


class Links:
    def __init__(self):
        self.dp_size = lax.axis_size("dp")
        self.hi_size = self.dp_size // 4
        index = lax.axis_index("dp")
        self.core = index & 1
        self.at = {"lo": (index >> 1) & 1, "tensor": lax.axis_index("tensor")}
        self.hi = index >> 2

    def over_dp(self, v, mask):
        return lax.ppermute(v, "dp", [(i, i ^ mask) for i in range(self.dp_size)])

    def swap(self, v, axis):
        if axis == "tensor":
            return lax.ppermute(v, "tensor", [(0, 1), (1, 0)])
        return self.over_dp(v, {"core": 1, "lo": 2}[axis])

    def over_hi(self, v, distance):
        return self.over_dp(v, 4 * distance)


def place_kernel(order, where, mine_ref, other_ref, *out_refs):
    hi_size = mine_ref.shape[2]

    def step(distance, carry):
        for i in range(2):
            for j in range(2):
                at = dict(zip(order, (where[0 if order[0] == "lo" else 1] ^ j, where[0 if order[1] == "lo" else 1] ^ i)))
                base = ((where[2] ^ distance) * 2 + at["lo"]) * 2
                for w, out_ref in enumerate(out_refs):
                    out_ref[at["tensor"], base + where[3]] = mine_ref[i, j, distance, w]
                    out_ref[at["tensor"], base + (1 - where[3])] = other_ref[i, j, distance, w]
        return carry

    lax.fori_loop(0, hi_size, step, 0)


def gather_tree(links, shards_in, order):
    stage = jnp.stack(shards_in)[None]
    stage = jnp.concatenate([stage] + [links.over_hi(stage, d) for d in range(1, links.hi_size)], 0)
    for axis in order:
        stage = jnp.stack([stage, links.swap(stage, axis)])
    other = links.swap(stage, "core")
    rows, columns = shards_in[0].shape
    where = jnp.stack([links.at["lo"], links.at["tensor"], links.hi, links.core]).astype(jnp.int32)
    blocks = links.dp_size
    full = pl.BlockSpec(memory_space=pltpu.VMEM)
    placed = pl.pallas_call(
        functools.partial(place_kernel, order),
        in_specs=[pl.BlockSpec(memory_space=pltpu.SMEM), full, full],
        out_specs=[full] * len(shards_in),
        out_shape=[jax.ShapeDtypeStruct((2, blocks, rows, columns), BF)] * len(shards_in),
        compiler_params=pltpu.CompilerParams(vmem_limit_bytes=48 * 1024 * 1024),
        cost_estimate=pl.CostEstimate(flops=0, bytes_accessed=4 * stage.size * 2, transcendentals=0),
        name="place_shards",
    )(where, stage, other)
    return [p.reshape(2, blocks * rows, columns) for p in placed]


def pick(v, index, axis=0):
    return lax.dynamic_index_in_dim(v, index, axis, keepdims=False)


def add_low(a, b):
    return (a.astype(F32) + b.astype(F32)).astype(BF)


def scatter_tree(links, parts, order):
    blocks = [[g.reshape(links.hi_size, 2, 2, -1, g.shape[1]) for g in half] for half in parts]

    def side(core):
        return jnp.stack([jnp.stack([pick(g, core, 2) for g in half]) for half in blocks])

    total = add_low(side(links.core), links.swap(side(1 - links.core), "core"))
    axes = ["tensor", "w", "hi", "lo"]
    for axis in order:
        at = axes.index(axis)
        here = links.at[axis]
        total = add_low(pick(total, here, at), links.swap(pick(total, 1 - here, at), axis))
        axes.pop(at)
    out = pick(total, links.hi, 1).astype(F32)
    for d in range(1, links.hi_size):
        out = out + links.over_hi(pick(total, links.hi ^ d, 1), d).astype(F32)
    return [out[w] for w in range(out.shape[0])]


def sum_everywhere(links, vec):
    first = vec + links.swap(vec, "tensor")
    vec = first
    bit = 1
    while bit < links.dp_size:
        vec = vec + links.over_dp(vec, bit)
        bit *= 2
    return vec, first


def split_vec(vec, sizes):
    out, at = [], 0
    for size in sizes:
        out.append(lax.slice_in_dim(vec, at, at + size))
        at += size
    return out


def shards(
    inputs,
    lengths,
    query_weight,
    key_weight,
    value_weight,
    query_bias,
    value_bias,
    out_weight,
    out_bias,
    first_gain,
    first_shift,
    input_projection_weight,
    input_projection_bias,
    output_projection_weight,
    output_projection_bias,
    second_gain,
    second_shift,
    out_cotangent,
):
    links = Links()
    half, seqs, _ = inputs.shape
    rows = half * seqs
    width = D // 2
    hidden_width = FF // 2
    tindex = jnp.reshape(links.at["tensor"], (1,)).astype(jnp.int32)
    everywhere = ("tensor", "dp")

    ffn_w = lax.all_gather(
        jnp.concatenate([input_projection_weight, output_projection_weight.T], 1), everywhere, axis=0, tiled=True
    ).reshape(2, D, 2 * hidden_width)
    up_w = [ffn_w[t, :, :hidden_width] for t in range(2)]
    down_w = [ffn_w[t, :, hidden_width:] for t in range(2)]
    inputs_seq = inputs.transpose(1, 0, 2).reshape(rows, D)
    rows_low = inputs_seq.astype(BF)
    query_w, key_w = gather_tree(links, [query_weight, key_weight], ("tensor", "lo"))
    value_w, out_w = gather_tree(links, [value_weight, out_weight.T], ("lo", "tensor"))
    rows_both = jnp.stack([rows_low, links.swap(rows_low, "tensor")])
    rows_flat = rows_both.reshape(2 * rows, D)
    queries, keys, values, context, log_sums = [], [], [], [], []
    for t in range(2):
        part = slice(t * width, (t + 1) * width)
        queries.append((dot(rows_low, query_w[t], 1, 0) + query_bias[part]).astype(BF) * jnp.array(HD**-0.5, BF))
        keys.append(dot(rows_flat, key_w[t], 1, 0).astype(BF).reshape(2, rows, width))
        values.append((dot(rows_flat, value_w[t], 1, 0) + value_bias[part]).astype(BF).reshape(2, rows, width))
        ctx, lse = attend_forward(lengths, tindex, queries[t], keys[t], values[t], seqs)
        context.append(ctx)
        log_sums.append(lse)
    attention = dot(context[0], out_w[0], 1, 1) + dot(context[1], out_w[1], 1, 1)
    hidden, normed_one, inv_one = layer_norm(inputs_seq + attention + out_bias, first_gain, first_shift)
    hidden_low = hidden.astype(BF)
    acts, slopes = [], []
    for t in range(2):
        pre = dot(hidden_low, up_w[t], 1, 0) + input_projection_bias[t * hidden_width : (t + 1) * hidden_width]
        act, slope = gelu_both(pre)
        acts.append(act.astype(BF))
        slopes.append(slope.astype(BF))
    branch = dot(acts[0], down_w[0], 1, 1) + dot(acts[1], down_w[1], 1, 1)
    outputs, normed_two, inv_two = layer_norm(
        hidden + branch + output_projection_bias, second_gain, second_shift
    )
    cotangent = out_cotangent.transpose(1, 0, 2).reshape(rows, D)
    second_grad = norm_back(cotangent, normed_two, inv_two, second_gain)
    second_gain_part = jnp.sum(cotangent * normed_two, axis=0)
    second_shift_part = jnp.sum(cotangent, axis=0)
    down_bias_part = jnp.sum(second_grad, axis=0)
    second_low = second_grad.astype(BF)
    (down_sum,) = scatter_tree(
        links, [[dot(second_low, acts[t], 0, 0).astype(BF)] for t in range(2)], ("tensor", "lo")
    )
    pre_grads, up_bias_parts = [], []
    for t in range(2):
        pre_grad = (dot(second_low, down_w[t], 1, 0) * slopes[t].astype(F32)).astype(BF)
        pre_grads.append(pre_grad)
        up_bias_parts.append(jnp.sum(pre_grad, axis=0, dtype=F32))
    (up_sum,) = scatter_tree(
        links, [[dot(hidden_low, pre_grads[t], 0, 0).astype(BF)] for t in range(2)], ("lo", "tensor")
    )
    hidden_grad = second_grad + (dot(pre_grads[0], up_w[0], 1, 1) + dot(pre_grads[1], up_w[1], 1, 1))
    first_grad = norm_back(hidden_grad, normed_one, inv_one, first_gain)
    first_gain_part = jnp.sum(hidden_grad * normed_one, axis=0)
    first_shift_part = jnp.sum(hidden_grad, axis=0)
    out_bias_part = jnp.sum(first_grad, axis=0)
    first_low = first_grad.astype(BF)
    early, _ = sum_everywhere(
        links,
        jnp.concatenate(
            [
                out_bias_part,
                first_gain_part,
                first_shift_part,
                down_bias_part,
                second_gain_part,
                second_shift_part,
                *up_bias_parts,
            ]
        ),
    )
    out_bias_sum, first_gain_sum, first_shift_sum, down_bias_sum, second_gain_sum, second_shift_sum, up_bias_sum = (
        split_vec(early, [D] * 6 + [FF])
    )
    query_grads, key_grads, value_grads = [], [], []
    for t in range(2):
        context_grad = dot(first_low, out_w[t], 1, 0).astype(BF)
        dq, dk, dv = attend_backward(
            lengths, tindex, queries[t], keys[t], values[t], context[t], log_sums[t], context_grad, seqs
        )
        query_grads.append(dq)
        key_grads.append(dk)
        value_grads.append(dv)
    late, late_first = sum_everywhere(
        links,
        jnp.concatenate(
            [jnp.sum(g, axis=0, dtype=F32) for g in query_grads]
            + [jnp.sum(g, axis=(0, 1), dtype=F32) for g in value_grads]
        ),
    )
    query_bias_sum, value_bias_sum = split_vec(late, [D, D])

    def back(side):
        return sum(dot(key_grads[t][side], key_w[t], 1, 1) + dot(value_grads[t][side], value_w[t], 1, 1) for t in range(2))

    other_total, _ = lax.optimization_barrier((back(1).astype(BF), late_first))
    from_other = links.swap(other_total, "tensor")
    own_total = back(0) + (dot(query_grads[0], query_w[0], 1, 1) + dot(query_grads[1], query_w[1], 1, 1))
    input_grad = first_grad + (own_total + from_other.astype(F32))
    query_key_parts, value_out_parts = [], []
    for t in range(2):
        query_key_parts.append(
            [
                dot(rows_low, query_grads[t], 0, 0).astype(BF),
                dot(rows_flat, key_grads[t].reshape(2 * rows, width), 0, 0).astype(BF),
            ]
        )
        value_out_parts.append(
            [
                dot(rows_flat, value_grads[t].reshape(2 * rows, width), 0, 0).astype(BF),
                dot(first_low, context[t], 0, 0).astype(BF),
            ]
        )
    query_sum, key_sum = scatter_tree(links, query_key_parts, ("lo", "tensor"))
    value_sum, out_sum = scatter_tree(links, value_out_parts, ("lo", "tensor"))

    def positions_first(v):
        return v.reshape(seqs, half, D).transpose(1, 0, 2)

    return (
        positions_first(outputs),
        positions_first(input_grad),
        query_sum,
        key_sum,
        value_sum,
        query_bias_sum,
        value_bias_sum,
        out_sum.T,
        out_bias_sum,
        first_gain_sum,
        first_shift_sum,
        up_sum,
        up_bias_sum,
        down_sum.T,
        down_bias_sum,
        second_gain_sum,
        second_shift_sum,
    )


def solution(mesh):
    in_specs = (
        P("tensor", "dp", None),
        P("dp"),
        P("dp", "tensor"),
        P("dp", "tensor"),
        P("dp", "tensor"),
        P(),
        P(),
        P("tensor", "dp"),
        P(),
        P(),
        P(),
        P("dp", "tensor"),
        P(),
        P("tensor", "dp"),
        P(),
        P(),
        P(),
        P("tensor", "dp", None),
    )
    out_specs = (
        P("tensor", "dp", None),
        P("tensor", "dp", None),
        P("dp", "tensor"),
        P("dp", "tensor"),
        P("dp", "tensor"),
        P(),
        P(),
        P("tensor", "dp"),
        P(),
        P(),
        P(),
        P("dp", "tensor"),
        P(),
        P("tensor", "dp"),
        P(),
        P(),
        P(),
    )
    return jax.shard_map(shards, mesh=mesh, in_specs=in_specs, out_specs=out_specs, check_vma=False)
```

```python
import functools

import jax
import jax.numpy as jnp
from jax import lax
from jax.experimental import pallas as pl
from jax.experimental.pallas import tpu as pltpu
from jax.sharding import PartitionSpec as P

D = 768
H = 12
HD = 64
FF = 3072

NORM_EPSILON = 1e-12
BF = jnp.bfloat16
F32 = jnp.float32


def dot(a, b, da, db):
    return lax.dot_general(a, b, (((da,), (db,)), ((), ())), preferred_element_type=F32)


def layer_norm(resid, gain_vec, shift_vec):
    mean_value = jnp.mean(resid, -1, keepdims=True)
    centred = resid - mean_value
    variance = jnp.mean(centred * centred, -1, keepdims=True)
    inv_std = lax.rsqrt(variance + NORM_EPSILON)
    normed = centred * inv_std
    return (normed * gain_vec + shift_vec, normed, inv_std)


def norm_back(grad_in, normed, inv_std, gain_vec):
    scaled = grad_in * gain_vec
    return inv_std * (
        scaled
        - jnp.mean(scaled, -1, keepdims=True)
        - normed * jnp.mean(scaled * normed, -1, keepdims=True)
    )


def gelu_both(v):
    z = jnp.abs(v) * (0.5**0.5)
    t = 1.0 / (1.0 + 0.3275911 * z)
    gauss = jnp.exp(-0.5 * v * v)
    poly = t * (
        0.5 * 0.254829592
        + t * (0.5 * -0.284496736 + t * (0.5 * 1.421413741 + t * (0.5 * -1.453152027 + t * (0.5 * 1.061405429))))
    )
    tail = poly * gauss
    phi_cum = jnp.where(v < 0, tail, 1.0 - tail)
    return v * phi_cum, phi_cum + v * gauss * 0.3989422804014327


def mask_bias(half, axis, length, place):
    shape = (1, half) if axis else (half, 1)
    at = lax.broadcasted_iota(jnp.int32, shape, axis)
    parts = [jnp.where(at + p * half < length, 0.0, -1e30) for p in (place, 1 - place)]
    return jnp.concatenate(parts, axis)


def attend_forward_kernel(heads, half, lens, tindex, q_ref, k_ref, v_ref, ctx_ref, lse_ref):
    bias = mask_bias(half, 1, lens[pl.program_id(0)], tindex[0])
    col = lax.broadcasted_iota(jnp.int32, (half, 128), 1)
    lse_tile = jnp.zeros((half, 128), F32)
    for h in range(heads):
        sl = slice(h * HD, (h + 1) * HD)
        k = k_ref[:, :, sl].reshape(2 * half, HD)
        v = v_ref[:, :, sl].reshape(2 * half, HD)
        s = dot(q_ref[:, sl], k, 1, 1) + bias
        m = jnp.max(s, -1, keepdims=True)
        e = jnp.exp(s - m)
        total = jnp.sum(e, -1, keepdims=True)
        ctx_ref[:, sl] = (dot(e.astype(BF), v, 1, 0) / total).astype(BF)
        lse_tile = jnp.where(col == h, m + jnp.log(total), lse_tile)
    lse_ref[0] = lse_tile


def attend_backward_kernel(
    heads, half, lens, tindex, q_ref, k_ref, v_ref, ctx_ref, lse_ref, dctx_ref, *rest
):
    dq_ref, dk_ref, dv_ref, sums_ref = rest[-4:]
    bias = mask_bias(half, 0, lens[pl.program_id(0)], tindex[0])
    lse_rows = jnp.transpose(lse_ref[0])
    prod = ctx_ref[...].astype(F32) * dctx_ref[...].astype(F32)
    col = lax.broadcasted_iota(jnp.int32, (half, 128), 1)
    delta_tile = jnp.zeros((half, 128), F32)
    for h in range(heads):
        delta_tile = jnp.where(
            col == h, jnp.sum(prod[:, h * HD : (h + 1) * HD], -1, keepdims=True), delta_tile
        )
    delta_rows = jnp.transpose(delta_tile)
    for h in range(heads):
        sl = slice(h * HD, (h + 1) * HD)
        q = q_ref[:, sl]
        dc = dctx_ref[:, sl]
        k = k_ref[:, :, sl].reshape(2 * half, HD)
        v = v_ref[:, :, sl].reshape(2 * half, HD)
        p = jnp.exp(dot(k, q, 1, 1) + bias - lse_rows[h : h + 1, :])
        ds = (p * (dot(v, dc, 1, 1) - delta_rows[h : h + 1, :])).astype(BF)
        dk_ref[:, :, sl] = dot(ds, q, 1, 0).astype(BF).reshape(2, half, HD)
        dv = dot(p.astype(BF), dc, 1, 0).astype(BF)
        dv_ref[:, :, sl] = dv.reshape(2, half, HD)
        dq = (dot(ds, k, 0, 0) * HD**-0.5).astype(BF)
        dq_ref[:, sl] = dq
        sums_ref[0, 0:1, sl] = jnp.sum(dq.astype(F32), 0, keepdims=True)
        sums_ref[0, 1:2, sl] = jnp.sum(dv.astype(F32), 0, keepdims=True)


def attend_specs(half, width):
    rows = pl.BlockSpec((half, width), lambda s, *_: (s, 0))
    pair = pl.BlockSpec((2, half, width), lambda s, *_: (0, s, 0))
    stat = pl.BlockSpec((1, half, 128), lambda s, *_: (s, 0, 0))
    return rows, pair, stat


def attend_forward(lengths, tindex, q, k, v, seqs):
    rows, width = q.shape
    half = rows // seqs
    flat, pair, stat = attend_specs(half, width)
    return pl.pallas_call(
        functools.partial(attend_forward_kernel, width // HD, half),
        grid_spec=pltpu.PrefetchScalarGridSpec(
            num_scalar_prefetch=2, grid=(seqs,), in_specs=[flat, pair, pair], out_specs=[flat, stat]
        ),
        out_shape=[
            jax.ShapeDtypeStruct((rows, width), BF),
            jax.ShapeDtypeStruct((seqs, half, 128), F32),
        ],
        compiler_params=pltpu.CompilerParams(vmem_limit_bytes=24 * 1024 * 1024),
        cost_estimate=pl.CostEstimate(flops=8_000_000_000, bytes_accessed=5_000_000, transcendentals=3_500_000),
        name="attend_forward",
    )(lengths, tindex, q, k, v)


def attend_backward(lengths, tindex, q, k, v, ctx, lse, dctx, seqs, after):
    rows, width = q.shape
    half = rows // seqs
    flat, pair, stat = attend_specs(half, width)
    dq, dk, dv, sums = pl.pallas_call(
        functools.partial(attend_backward_kernel, width // HD, half),
        grid_spec=pltpu.PrefetchScalarGridSpec(
            num_scalar_prefetch=2,
            grid=(seqs,),
            in_specs=[flat, pair, pair, flat, stat, flat] + [pl.BlockSpec(memory_space=pl.ANY)] * len(after),
            out_specs=[flat, pair, pair, pl.BlockSpec((1, 2, width), lambda s, *_: (s, 0, 0))],
        ),
        out_shape=[
            jax.ShapeDtypeStruct((rows, width), BF),
            jax.ShapeDtypeStruct((2, rows, width), BF),
            jax.ShapeDtypeStruct((2, rows, width), BF),
            jax.ShapeDtypeStruct((seqs, 2, width), F32),
        ],
        compiler_params=pltpu.CompilerParams(vmem_limit_bytes=24 * 1024 * 1024),
        cost_estimate=pl.CostEstimate(flops=18_000_000_000, bytes_accessed=10_000_000, transcendentals=3_500_000),
        name="attend_backward",
    )(lengths, tindex, q, k, v, ctx, lse, dctx, *after)
    return dq, dk, dv, jnp.sum(sums, 0)


def back_kernel(count, has_base, *refs):
    out_ref = refs[-1]
    total = refs[2 * count][...] if has_base else None
    for i in range(count):
        g = refs[i][...].reshape(out_ref.shape[0], -1)
        part = dot(g, refs[count + i][0], 1, 1)
        total = part if total is None else total + part
    out_ref[...] = total.astype(out_ref.dtype)


def back_product(terms, base, dtype, seqs, after):
    block = (base if base is not None else terms[0][0]).shape[-2] // seqs
    specs, weight_specs = [], []
    for grad, side, weight, t in terms:
        if side is None:
            specs.append(pl.BlockSpec((block, grad.shape[1]), lambda i: (i, 0)))
        else:
            specs.append(pl.BlockSpec((1, block, grad.shape[2]), lambda i, side=side: (side, i, 0)))
        weight_specs.append(pl.BlockSpec((1,) + weight.shape[1:], lambda i, t=t: (t, 0, 0)))
    out_spec = pl.BlockSpec((block, D), lambda i: (i, 0))
    args = [x[0] for x in terms] + [x[2] for x in terms] + ([base] if base is not None else [])
    return pl.pallas_call(
        functools.partial(back_kernel, len(terms), base is not None),
        grid=(seqs,),
        in_specs=specs
        + weight_specs
        + ([out_spec] if base is not None else [])
        + [pl.BlockSpec(memory_space=pl.ANY)] * len(after),
        out_specs=out_spec,
        out_shape=jax.ShapeDtypeStruct((block * seqs, D), dtype),
        compiler_params=pltpu.CompilerParams(vmem_limit_bytes=32 * 1024 * 1024),
        cost_estimate=pl.CostEstimate(
            flops=sum(2 * block * seqs * w.shape[1] * w.shape[2] for _, _, w, _ in terms),
            bytes_accessed=8_000_000,
            transcendentals=0,
        ),
        name="back_product",
    )(*args, *after)


def weight_kernel(core, own_ref, oth_ref, first_ref, dq_ref, dk_ref, dv_ref, ctx_ref, *rest):
    keep_ref, send_ref = rest[-2:]
    _, blocks, rows, columns = keep_ref.shape
    own = jnp.transpose(own_ref[...])
    oth = jnp.transpose(oth_ref[...])
    first = core[0] == 0

    def put(w, full):
        full = full.astype(BF).reshape(blocks, 2, rows, columns)
        keep_ref[w] = jnp.where(first, full[:, 0], full[:, 1])
        send_ref[w] = jnp.where(first, full[:, 1], full[:, 0])

    put(0, dot(own, dq_ref[...], 1, 0))
    put(1, dot(own, dk_ref[0], 1, 0) + dot(oth, dk_ref[1], 1, 0))
    put(2, dot(own, dv_ref[0], 1, 0) + dot(oth, dv_ref[1], 1, 0))
    put(3, dot(jnp.transpose(first_ref[...]), ctx_ref[...], 1, 0))


def weight_products(links, own, oth, first_low, dq, dk, dv, ctx, after):
    rows = D // links.dp_size
    columns = dq.shape[-1]
    if rows % 16:
        both = jnp.concatenate([own, oth], 0)
        parts = [
            dot(own, dq, 0, 0),
            dot(both, dk.reshape(-1, columns), 0, 0),
            dot(both, dv.reshape(-1, columns), 0, 0),
            dot(first_low, ctx, 0, 0),
        ]
        return halve_cores(links, [[p.astype(BF) for p in parts]])[0], parts[0]
    shape = (4, links.dp_size // 2, rows, columns)
    full = pl.BlockSpec(memory_space=pltpu.VMEM)
    keep, send = pl.pallas_call(
        weight_kernel,
        in_specs=[pl.BlockSpec(memory_space=pltpu.SMEM)]
        + [full] * 7
        + [pl.BlockSpec(memory_space=pl.ANY)] * len(after),
        out_specs=[full, full],
        out_shape=[jax.ShapeDtypeStruct(shape, BF)] * 2,
        compiler_params=pltpu.CompilerParams(vmem_limit_bytes=40 * 1024 * 1024),
        cost_estimate=pl.CostEstimate(
            flops=2 * D * columns * own.shape[0] * 6, bytes_accessed=10_000_000, transcendentals=0
        ),
        name="weight_products",
    )(links.core.reshape(1).astype(jnp.int32), own, oth, first_low, dq, dk, dv, ctx, *after)
    total = add_low(keep, links.swap(send, "core"))
    return total.reshape(4, links.hi_size, 2, rows, columns), keep


def project_kernel(
    own_ref, oth_ref, qw_ref, kw_ref, vw_ref, qb_ref, vb_ref, q0, q1, k0, k1, v0, v1
):
    own, oth = own_ref[...], oth_ref[...]
    for t, (q, k, v) in enumerate(((q0, k0, v0), (q1, k1, v1))):
        q[...] = ((dot(own, qw_ref[t], 1, 0) + qb_ref[t]).astype(BF) * jnp.array(HD**-0.5, BF)).astype(BF)
        for i, x in enumerate((own, oth)):
            k[i] = dot(x, kw_ref[t], 1, 0).astype(BF)
            v[i] = (dot(x, vw_ref[t], 1, 0) + vb_ref[t]).astype(BF)


def project(own, oth, query_w, key_w, value_w, query_bias, value_bias, seqs):
    rows, width = own.shape[0], query_w.shape[2]
    half = rows // seqs
    full = pl.BlockSpec(memory_space=pltpu.VMEM)
    flat = pl.BlockSpec((half, width), lambda i: (i, 0))
    pair = pl.BlockSpec((2, half, width), lambda i: (0, i, 0))
    q0, q1, k0, k1, v0, v1 = pl.pallas_call(
        project_kernel,
        grid=(seqs,),
        in_specs=[pl.BlockSpec((half, D), lambda i: (i, 0))] * 2 + [full] * 5,
        out_specs=[flat, flat, pair, pair, pair, pair],
        out_shape=[jax.ShapeDtypeStruct((rows, width), BF)] * 2 + [jax.ShapeDtypeStruct((2, rows, width), BF)] * 4,
        compiler_params=pltpu.CompilerParams(vmem_limit_bytes=32 * 1024 * 1024),
        cost_estimate=pl.CostEstimate(flops=2 * 10 * rows * D * width, bytes_accessed=16_000_000, transcendentals=0),
        name="project",
    )(
        own,
        oth,
        query_w,
        key_w,
        value_w,
        query_bias.reshape(2, 1, width),
        value_bias.reshape(2, 1, width),
    )
    return [q0, q1], [k0, k1], [v0, v1]


def pack_kernel(count, *refs):
    for i in range(count):
        refs[-1][i] = refs[i][...]


def pack(arrays, after):
    full = pl.BlockSpec(memory_space=pltpu.VMEM)
    return pl.pallas_call(
        functools.partial(pack_kernel, len(arrays)),
        in_specs=[full] * len(arrays) + [pl.BlockSpec(memory_space=pl.ANY)] * len(after),
        out_specs=full,
        out_shape=jax.ShapeDtypeStruct((len(arrays),) + arrays[0].shape, arrays[0].dtype),
        name="pack_shards",
    )(*arrays, *after)


class Links:
    def __init__(self):
        self.dp_size = lax.axis_size("dp")
        self.hi_size = self.dp_size // 4
        index = lax.axis_index("dp")
        self.core = index & 1
        self.at = {"lo": (index >> 1) & 1, "tensor": lax.axis_index("tensor")}
        self.hi = index >> 2

    def over_dp(self, v, mask):
        return lax.ppermute(v, "dp", [(i, i ^ mask) for i in range(self.dp_size)])

    def swap(self, v, axis):
        if axis == "tensor":
            return lax.ppermute(v, "tensor", [(0, 1), (1, 0)])
        return self.over_dp(v, {"core": 1, "lo": 2}[axis])

    def over_hi(self, v, distance):
        return self.over_dp(v, 4 * distance)


def place_kernel(order, where, mine_ref, other_ref, *out_refs):
    hi_size = mine_ref.shape[2]

    def step(distance, carry):
        for i in range(2):
            for j in range(2):
                at = dict(zip(order, (where[0 if order[0] == "lo" else 1] ^ j, where[0 if order[1] == "lo" else 1] ^ i)))
                base = ((where[2] ^ distance) * 2 + at["lo"]) * 2
                for w, out_ref in enumerate(out_refs):
                    out_ref[at["tensor"], base + where[3]] = mine_ref[i, j, distance, w]
                    out_ref[at["tensor"], base + (1 - where[3])] = other_ref[i, j, distance, w]
        return carry

    lax.fori_loop(0, hi_size, step, 0)


def gather_tree(links, shards_in, order, after):
    stage = pack(shards_in, after[0])
    stage = pack([stage] + [links.over_hi(stage, d) for d in range(1, links.hi_size)], after[1])
    stage = jnp.stack([stage, links.swap(stage, order[0])])
    stage = jnp.stack([stage, links.swap(stage, order[1])])
    other = links.swap(stage, "core")
    rows, columns = shards_in[0].shape
    where = jnp.stack([links.at["lo"], links.at["tensor"], links.hi, links.core]).astype(jnp.int32)
    blocks = links.dp_size
    full = pl.BlockSpec(memory_space=pltpu.VMEM)
    placed = pl.pallas_call(
        functools.partial(place_kernel, order),
        in_specs=[pl.BlockSpec(memory_space=pltpu.SMEM), full, full],
        out_specs=[full] * len(shards_in),
        out_shape=[jax.ShapeDtypeStruct((2, blocks, rows, columns), BF)] * len(shards_in),
        compiler_params=pltpu.CompilerParams(vmem_limit_bytes=48 * 1024 * 1024),
        cost_estimate=pl.CostEstimate(flops=0, bytes_accessed=4 * stage.size * 2, transcendentals=0),
        name="place_shards",
    )(where, stage, other)
    return [p.reshape(2, blocks * rows, columns) for p in placed]


def pick(v, index, axis=0):
    return lax.dynamic_index_in_dim(v, index, axis, keepdims=False)


def add_low(a, b):
    return (a.astype(F32) + b.astype(F32)).astype(BF)


def halve_cores(links, parts):
    blocks = [[g.reshape(links.hi_size, 2, 2, -1, g.shape[1]) for g in half] for half in parts]

    def side(core):
        return jnp.stack([jnp.stack([pick(g, core, 2) for g in half]) for half in blocks])

    return add_low(side(links.core), links.swap(side(1 - links.core), "core"))


def halve(links, total, axis, at):
    here = links.at[axis]
    return add_low(pick(total, here, at), links.swap(pick(total, 1 - here, at), axis))


def finish(links, total):
    out = pick(total, links.hi, 1).astype(F32)
    for d in range(1, links.hi_size):
        out = out + links.over_hi(pick(total, links.hi ^ d, 1), d).astype(F32)
    return [out[w] for w in range(out.shape[0])]


def sum_everywhere(links, vec):
    vec = vec + links.swap(vec, "tensor")
    bit = 1
    while bit < links.dp_size:
        vec = vec + links.over_dp(vec, bit)
        bit *= 2
    return vec


def split_vec(vec, sizes):
    out, at = [], 0
    for size in sizes:
        out.append(lax.slice_in_dim(vec, at, at + size))
        at += size
    return out


def shards(
    inputs,
    lengths,
    query_weight,
    key_weight,
    value_weight,
    query_bias,
    value_bias,
    out_weight,
    out_bias,
    first_gain,
    first_shift,
    input_projection_weight,
    input_projection_bias,
    output_projection_weight,
    output_projection_bias,
    second_gain,
    second_shift,
    out_cotangent,
):
    links = Links()
    half, seqs, _ = inputs.shape
    rows = half * seqs
    width = D // 2
    hidden_width = FF // 2
    tindex = jnp.reshape(links.at["tensor"], (1,)).astype(jnp.int32)
    everywhere = ("tensor", "dp")

    ffn_w = lax.all_gather(
        jnp.concatenate([input_projection_weight, output_projection_weight.T], 1), everywhere, axis=0, tiled=True
    ).reshape(2, D, 2 * hidden_width)
    up_w = [ffn_w[t, :, :hidden_width] for t in range(2)]
    down_w = [ffn_w[t, :, hidden_width:] for t in range(2)]
    inputs_seq = inputs.transpose(1, 0, 2).reshape(rows, D)
    rows_low = inputs_seq.astype(BF)
    rows_other = links.swap(rows_low, "tensor")
    query_w, key_w = gather_tree(links, [query_weight, key_weight], ("tensor", "lo"), [[rows_low], [rows_other]])
    value_w, out_w = gather_tree(links, [value_weight, out_weight.T], ("lo", "tensor"), [[rows_low], []])
    queries, keys, values = project(rows_low, rows_other, query_w, key_w, value_w, query_bias, value_bias, seqs)
    context, log_sums = [], []
    for t in range(2):
        ctx, lse = attend_forward(lengths, tindex, queries[t], keys[t], values[t], seqs)
        context.append(ctx)
        log_sums.append(lse)
    attention = dot(context[0], out_w[0], 1, 1) + dot(context[1], out_w[1], 1, 1)
    hidden, normed_one, inv_one = layer_norm(inputs_seq + attention + out_bias, first_gain, first_shift)
    hidden_low = hidden.astype(BF)
    acts, slopes = [], []
    for t in range(2):
        pre = dot(hidden_low, up_w[t], 1, 0) + input_projection_bias[t * hidden_width : (t + 1) * hidden_width]
        act, slope = gelu_both(pre)
        acts.append(act.astype(BF))
        slopes.append(lax.optimization_barrier(slope.astype(BF)))
    branch = dot(acts[0], down_w[0], 1, 1) + dot(acts[1], down_w[1], 1, 1)
    outputs, normed_two, inv_two = layer_norm(
        hidden + branch + output_projection_bias, second_gain, second_shift
    )
    cotangent = out_cotangent.transpose(1, 0, 2).reshape(rows, D)
    second_grad = norm_back(cotangent, normed_two, inv_two, second_gain)
    second_gain_part = jnp.sum(cotangent * normed_two, axis=0)
    second_shift_part = jnp.sum(cotangent, axis=0)
    down_bias_part = jnp.sum(second_grad, axis=0)
    second_low = second_grad.astype(BF)
    down_chip = halve_cores(links, [[dot(second_low, acts[t], 0, 0).astype(BF)] for t in range(2)])
    pre_grads, up_bias_parts = [], []
    for t in range(2):
        pre_grad = (dot(second_low, down_w[t], 1, 0) * slopes[t].astype(F32)).astype(BF)
        pre_grads.append(pre_grad)
        up_bias_parts.append(jnp.sum(pre_grad, axis=0, dtype=F32))
    up_chip = halve_cores(links, [[dot(hidden_low, pre_grads[t], 0, 0).astype(BF)] for t in range(2)])
    hidden_grad = second_grad + (dot(pre_grads[0], up_w[0], 1, 1) + dot(pre_grads[1], up_w[1], 1, 1))
    first_grad = norm_back(hidden_grad, normed_one, inv_one, first_gain)
    first_gain_part = jnp.sum(hidden_grad * normed_one, axis=0)
    first_shift_part = jnp.sum(hidden_grad, axis=0)
    out_bias_part = jnp.sum(first_grad, axis=0)
    first_low = first_grad.astype(BF)
    down_half = halve(links, down_chip, "tensor", 0)
    up_half = halve(links, up_chip, "lo", 3)
    query_grads, key_grads, value_grads, bias_parts, chip = [], [], [], [], []
    down_quarter = halve(links, down_half, "lo", 2)
    up_quarter = halve(links, up_half, "tensor", 0)
    after = [down_chip, up_chip]
    for t in range(2):
        context_grad = dot(first_low, out_w[t], 1, 0).astype(BF)
        dq, dk, dv, sums = attend_backward(
            lengths, tindex, queries[t], keys[t], values[t], context[t], log_sums[t], context_grad, seqs, after
        )
        query_grads.append(dq)
        key_grads.append(dk)
        value_grads.append(dv)
        bias_parts.append(sums)
        if t == 1:
            other_total = back_product(
                [(key_grads[i], 1, key_w, i) for i in range(2)] + [(value_grads[i], 1, value_w, i) for i in range(2)],
                None,
                BF,
                seqs,
                [chip[0]],
            )
            after = [other_total, down_quarter, up_quarter]
        total, made = weight_products(
            links, rows_low, rows_other, first_low, dq, dk, dv, context[t], after if t else []
        )
        chip.append(total)
        after = [down_half, up_half, made]
    from_other = links.swap(other_total, "tensor")
    chip_half = [halve(links, c, "lo", 2) for c in chip]
    vectors = jnp.concatenate(
            [
                out_bias_part,
                first_gain_part,
                first_shift_part,
                down_bias_part,
                second_gain_part,
                second_shift_part,
                *up_bias_parts,
                bias_parts[0][0],
                bias_parts[1][0],
                bias_parts[0][1],
                bias_parts[1][1],
            ]
        ).reshape(-1, 128)
    sums = sum_everywhere(links, pack([vectors], [chip[1], chip_half[0]])[0]).reshape(-1)
    (
        out_bias_sum,
        first_gain_sum,
        first_shift_sum,
        down_bias_sum,
        second_gain_sum,
        second_shift_sum,
        up_bias_sum,
        query_bias_sum,
        value_bias_sum,
    ) = split_vec(sums, [D] * 6 + [FF, D, D])
    own_total = back_product(
        [(query_grads[t], None, query_w, t) for t in range(2)]
        + [(key_grads[t], 0, key_w, t) for t in range(2)]
        + [(value_grads[t], 0, value_w, t) for t in range(2)],
        first_grad,
        F32,
        seqs,
        [],
    )
    input_grad = own_total + from_other.astype(F32)
    (down_sum,) = finish(links, down_quarter)
    (up_sum,) = finish(links, up_quarter)
    first_side = links.at["tensor"] == 0
    mine = jnp.where(first_side, chip_half[0], chip_half[1])
    theirs = jnp.where(first_side, chip_half[1], chip_half[0])
    query_sum, key_sum, value_sum, out_sum = finish(
        links, add_low(mine, links.swap(pack([theirs], [from_other])[0], "tensor"))
    )

    def positions_first(v):
        return v.reshape(seqs, half, D).transpose(1, 0, 2)

    return (
        positions_first(outputs),
        positions_first(input_grad),
        query_sum,
        key_sum,
        value_sum,
        query_bias_sum,
        value_bias_sum,
        out_sum.T,
        out_bias_sum,
        first_gain_sum,
        first_shift_sum,
        up_sum,
        up_bias_sum,
        down_sum.T,
        down_bias_sum,
        second_gain_sum,
        second_shift_sum,
    )


def solution(mesh):
    in_specs = (
        P("tensor", "dp", None),
        P("dp"),
        P("dp", "tensor"),
        P("dp", "tensor"),
        P("dp", "tensor"),
        P(),
        P(),
        P("tensor", "dp"),
        P(),
        P(),
        P(),
        P("dp", "tensor"),
        P(),
        P("tensor", "dp"),
        P(),
        P(),
        P(),
        P("tensor", "dp", None),
    )
    out_specs = (
        P("tensor", "dp", None),
        P("tensor", "dp", None),
        P("dp", "tensor"),
        P("dp", "tensor"),
        P("dp", "tensor"),
        P(),
        P(),
        P("tensor", "dp"),
        P(),
        P(),
        P(),
        P("dp", "tensor"),
        P(),
        P("tensor", "dp"),
        P(),
        P(),
        P(),
    )
    return jax.shard_map(shards, mesh=mesh, in_specs=in_specs, out_specs=out_specs, check_vma=False)
```

```python
import functools

import jax
import jax.numpy as jnp
from jax import lax
from jax.experimental import pallas as pl
from jax.experimental.pallas import tpu as pltpu
from jax.sharding import PartitionSpec as P

D = 768
H = 12
HD = 64
FF = 3072

NORM_EPSILON = 1e-12
BF = jnp.bfloat16
F32 = jnp.float32


def dot(a, b, da, db):
    return lax.dot_general(a, b, (((da,), (db,)), ((), ())), preferred_element_type=F32)


def layer_norm(resid, gain_vec, shift_vec):
    mean_value = jnp.mean(resid, -1, keepdims=True)
    centred = resid - mean_value
    variance = jnp.mean(centred * centred, -1, keepdims=True)
    inv_std = lax.rsqrt(variance + NORM_EPSILON)
    normed = centred * inv_std
    return (normed * gain_vec + shift_vec, normed, inv_std)


def norm_back(grad_in, normed, inv_std, gain_vec):
    scaled = grad_in * gain_vec
    return inv_std * (
        scaled
        - jnp.mean(scaled, -1, keepdims=True)
        - normed * jnp.mean(scaled * normed, -1, keepdims=True)
    )


def gelu_both(v):
    z = jnp.abs(v) * (0.5**0.5)
    t = 1.0 / (1.0 + 0.3275911 * z)
    gauss = jnp.exp(-0.5 * v * v)
    poly = t * (
        0.5 * 0.254829592
        + t * (0.5 * -0.284496736 + t * (0.5 * 1.421413741 + t * (0.5 * -1.453152027 + t * (0.5 * 1.061405429))))
    )
    tail = poly * gauss
    phi_cum = jnp.where(v < 0, tail, 1.0 - tail)
    return v * phi_cum, phi_cum + v * gauss * 0.3989422804014327


def mask_bias(half, axis, length, place):
    shape = (1, half) if axis else (half, 1)
    at = lax.broadcasted_iota(jnp.int32, shape, axis)
    parts = [jnp.where(at + p * half < length, 0.0, -1e30) for p in (place, 1 - place)]
    return jnp.concatenate(parts, axis)


def attend_forward_kernel(heads, half, lens, tindex, q_ref, k_ref, v_ref, ctx_ref, lse_ref):
    bias = mask_bias(half, 1, lens[pl.program_id(0)], tindex[0])
    col = lax.broadcasted_iota(jnp.int32, (half, 128), 1)
    lse_tile = jnp.zeros((half, 128), F32)
    for h in range(heads):
        sl = slice(h * HD, (h + 1) * HD)
        k = k_ref[:, :, sl].reshape(2 * half, HD)
        v = v_ref[:, :, sl].reshape(2 * half, HD)
        s = dot(q_ref[:, sl], k, 1, 1) + bias
        m = jnp.max(s, -1, keepdims=True)
        e = jnp.exp(s - m)
        total = jnp.sum(e, -1, keepdims=True)
        ctx_ref[:, sl] = (dot(e.astype(BF), v, 1, 0) / total).astype(BF)
        lse_tile = jnp.where(col == h, m + jnp.log(total), lse_tile)
    lse_ref[0] = lse_tile


def attend_backward_kernel(
    heads, half, lens, tindex, q_ref, k_ref, v_ref, ctx_ref, lse_ref, dctx_ref, *rest
):
    dq_ref, dk_ref, dv_ref, sums_ref = rest[-4:]
    bias = mask_bias(half, 0, lens[pl.program_id(0)], tindex[0])
    lse_rows = jnp.transpose(lse_ref[0])
    prod = ctx_ref[...].astype(F32) * dctx_ref[...].astype(F32)
    col = lax.broadcasted_iota(jnp.int32, (half, 128), 1)
    delta_tile = jnp.zeros((half, 128), F32)
    for h in range(heads):
        delta_tile = jnp.where(
            col == h, jnp.sum(prod[:, h * HD : (h + 1) * HD], -1, keepdims=True), delta_tile
        )
    delta_rows = jnp.transpose(delta_tile)
    for h in range(heads):
        sl = slice(h * HD, (h + 1) * HD)
        q = q_ref[:, sl]
        dc = dctx_ref[:, sl]
        k = k_ref[:, :, sl].reshape(2 * half, HD)
        v = v_ref[:, :, sl].reshape(2 * half, HD)
        p = jnp.exp(dot(k, q, 1, 1) + bias - lse_rows[h : h + 1, :])
        ds = (p * (dot(v, dc, 1, 1) - delta_rows[h : h + 1, :])).astype(BF)
        dk_ref[:, :, sl] = dot(ds, q, 1, 0).astype(BF).reshape(2, half, HD)
        dv = dot(p.astype(BF), dc, 1, 0).astype(BF)
        dv_ref[:, :, sl] = dv.reshape(2, half, HD)
        dq = (dot(ds, k, 0, 0) * HD**-0.5).astype(BF)
        dq_ref[:, sl] = dq
        sums_ref[0, 0:1, sl] = jnp.sum(dq.astype(F32), 0, keepdims=True)
        sums_ref[0, 1:2, sl] = jnp.sum(dv.astype(F32), 0, keepdims=True)


def attend_specs(half, width):
    rows = pl.BlockSpec((half, width), lambda s, *_: (s, 0))
    pair = pl.BlockSpec((2, half, width), lambda s, *_: (0, s, 0))
    stat = pl.BlockSpec((1, half, 128), lambda s, *_: (s, 0, 0))
    return rows, pair, stat


def attend_forward(lengths, tindex, q, k, v, seqs):
    rows, width = q.shape
    half = rows // seqs
    flat, pair, stat = attend_specs(half, width)
    return pl.pallas_call(
        functools.partial(attend_forward_kernel, width // HD, half),
        grid_spec=pltpu.PrefetchScalarGridSpec(
            num_scalar_prefetch=2, grid=(seqs,), in_specs=[flat, pair, pair], out_specs=[flat, stat]
        ),
        out_shape=[
            jax.ShapeDtypeStruct((rows, width), BF),
            jax.ShapeDtypeStruct((seqs, half, 128), F32),
        ],
        compiler_params=pltpu.CompilerParams(vmem_limit_bytes=24 * 1024 * 1024),
        cost_estimate=pl.CostEstimate(flops=8_000_000_000, bytes_accessed=5_000_000, transcendentals=3_500_000),
        name="attend_forward",
    )(lengths, tindex, q, k, v)


def attend_backward(lengths, tindex, q, k, v, ctx, lse, dctx, seqs, after):
    rows, width = q.shape
    half = rows // seqs
    flat, pair, stat = attend_specs(half, width)
    dq, dk, dv, sums = pl.pallas_call(
        functools.partial(attend_backward_kernel, width // HD, half),
        grid_spec=pltpu.PrefetchScalarGridSpec(
            num_scalar_prefetch=2,
            grid=(seqs,),
            in_specs=[flat, pair, pair, flat, stat, flat] + [pl.BlockSpec(memory_space=pl.ANY)] * len(after),
            out_specs=[flat, pair, pair, pl.BlockSpec((1, 2, width), lambda s, *_: (s, 0, 0))],
        ),
        out_shape=[
            jax.ShapeDtypeStruct((rows, width), BF),
            jax.ShapeDtypeStruct((2, rows, width), BF),
            jax.ShapeDtypeStruct((2, rows, width), BF),
            jax.ShapeDtypeStruct((seqs, 2, width), F32),
        ],
        compiler_params=pltpu.CompilerParams(vmem_limit_bytes=24 * 1024 * 1024),
        cost_estimate=pl.CostEstimate(flops=18_000_000_000, bytes_accessed=10_000_000, transcendentals=3_500_000),
        name="attend_backward",
    )(lengths, tindex, q, k, v, ctx, lse, dctx, *after)
    return dq, dk, dv, jnp.sum(sums, 0)


def back_kernel(count, has_base, *refs):
    out_ref = refs[-1]
    total = refs[2 * count][...] if has_base else None
    for i in range(count):
        g = refs[i][...].reshape(out_ref.shape[0], -1)
        part = dot(g, refs[count + i][0], 1, 1)
        total = part if total is None else total + part
    out_ref[...] = total.astype(out_ref.dtype)


def back_product(terms, base, dtype, seqs, after):
    block = (base if base is not None else terms[0][0]).shape[-2] // seqs
    specs, weight_specs = [], []
    for grad, side, weight, t in terms:
        if side is None:
            specs.append(pl.BlockSpec((block, grad.shape[1]), lambda i: (i, 0)))
        else:
            specs.append(pl.BlockSpec((1, block, grad.shape[2]), lambda i, side=side: (side, i, 0)))
        weight_specs.append(pl.BlockSpec((1,) + weight.shape[1:], lambda i, t=t: (t, 0, 0)))
    out_spec = pl.BlockSpec((block, D), lambda i: (i, 0))
    args = [x[0] for x in terms] + [x[2] for x in terms] + ([base] if base is not None else [])
    return pl.pallas_call(
        functools.partial(back_kernel, len(terms), base is not None),
        grid=(seqs,),
        in_specs=specs
        + weight_specs
        + ([out_spec] if base is not None else [])
        + [pl.BlockSpec(memory_space=pl.ANY)] * len(after),
        out_specs=out_spec,
        out_shape=jax.ShapeDtypeStruct((block * seqs, D), dtype),
        compiler_params=pltpu.CompilerParams(vmem_limit_bytes=32 * 1024 * 1024),
        cost_estimate=pl.CostEstimate(
            flops=sum(2 * block * seqs * w.shape[1] * w.shape[2] for _, _, w, _ in terms),
            bytes_accessed=8_000_000,
            transcendentals=0,
        ),
        name="back_product",
    )(*args, *after)


def weight_kernel(core, own_ref, oth_ref, first_ref, dq_ref, dk_ref, dv_ref, ctx_ref, *rest):
    keep_ref, send_ref = rest[-2:]
    _, blocks, rows, columns = keep_ref.shape
    own = jnp.transpose(own_ref[...])
    oth = jnp.transpose(oth_ref[...])
    first = core[0] == 0

    def put(w, full):
        full = full.astype(BF).reshape(blocks, 2, rows, columns)
        keep_ref[w] = jnp.where(first, full[:, 0], full[:, 1])
        send_ref[w] = jnp.where(first, full[:, 1], full[:, 0])

    put(0, dot(own, dq_ref[...], 1, 0))
    put(1, dot(own, dk_ref[0], 1, 0) + dot(oth, dk_ref[1], 1, 0))
    put(2, dot(own, dv_ref[0], 1, 0) + dot(oth, dv_ref[1], 1, 0))
    put(3, dot(jnp.transpose(first_ref[...]), ctx_ref[...], 1, 0))


def weight_products(links, own, oth, first_low, dq, dk, dv, ctx, after):
    rows = D // links.dp_size
    columns = dq.shape[-1]
    if rows % 16:
        both = jnp.concatenate([own, oth], 0)
        parts = [
            dot(own, dq, 0, 0),
            dot(both, dk.reshape(-1, columns), 0, 0),
            dot(both, dv.reshape(-1, columns), 0, 0),
            dot(first_low, ctx, 0, 0),
        ]
        return halve_cores(links, [[p.astype(BF) for p in parts]])[0], parts[0]
    shape = (4, links.dp_size // 2, rows, columns)
    full = pl.BlockSpec(memory_space=pltpu.VMEM)
    keep, send = pl.pallas_call(
        weight_kernel,
        in_specs=[pl.BlockSpec(memory_space=pltpu.SMEM)]
        + [full] * 7
        + [pl.BlockSpec(memory_space=pl.ANY)] * len(after),
        out_specs=[full, full],
        out_shape=[jax.ShapeDtypeStruct(shape, BF)] * 2,
        compiler_params=pltpu.CompilerParams(vmem_limit_bytes=40 * 1024 * 1024),
        cost_estimate=pl.CostEstimate(
            flops=2 * D * columns * own.shape[0] * 6, bytes_accessed=10_000_000, transcendentals=0
        ),
        name="weight_products",
    )(links.core.reshape(1).astype(jnp.int32), own, oth, first_low, dq, dk, dv, ctx, *after)
    total = add_low(keep, links.swap(send, "core"))
    return total.reshape(4, links.hi_size, 2, rows, columns), keep


def project_kernel(
    own_ref, oth_ref, qw_ref, kw_ref, vw_ref, qb_ref, vb_ref, q0, q1, k0, k1, v0, v1
):
    own, oth = own_ref[...], oth_ref[...]
    for t, (q, k, v) in enumerate(((q0, k0, v0), (q1, k1, v1))):
        q[...] = ((dot(own, qw_ref[t], 1, 0) + qb_ref[t]).astype(BF) * jnp.array(HD**-0.5, BF)).astype(BF)
        for i, x in enumerate((own, oth)):
            k[i] = dot(x, kw_ref[t], 1, 0).astype(BF)
            v[i] = (dot(x, vw_ref[t], 1, 0) + vb_ref[t]).astype(BF)


def project(own, oth, query_w, key_w, value_w, query_bias, value_bias, seqs):
    rows, width = own.shape[0], query_w.shape[2]
    half = rows // seqs
    full = pl.BlockSpec(memory_space=pltpu.VMEM)
    flat = pl.BlockSpec((half, width), lambda i: (i, 0))
    pair = pl.BlockSpec((2, half, width), lambda i: (0, i, 0))
    q0, q1, k0, k1, v0, v1 = pl.pallas_call(
        project_kernel,
        grid=(seqs,),
        in_specs=[pl.BlockSpec((half, D), lambda i: (i, 0))] * 2 + [full] * 5,
        out_specs=[flat, flat, pair, pair, pair, pair],
        out_shape=[jax.ShapeDtypeStruct((rows, width), BF)] * 2 + [jax.ShapeDtypeStruct((2, rows, width), BF)] * 4,
        compiler_params=pltpu.CompilerParams(vmem_limit_bytes=32 * 1024 * 1024),
        cost_estimate=pl.CostEstimate(flops=2 * 10 * rows * D * width, bytes_accessed=16_000_000, transcendentals=0),
        name="project",
    )(
        own,
        oth,
        query_w,
        key_w,
        value_w,
        query_bias.reshape(2, 1, width),
        value_bias.reshape(2, 1, width),
    )
    return [q0, q1], [k0, k1], [v0, v1]


def pack_kernel(count, *refs):
    for i in range(count):
        refs[-1][i] = refs[i][...]


def pack(arrays, after):
    full = pl.BlockSpec(memory_space=pltpu.VMEM)
    return pl.pallas_call(
        functools.partial(pack_kernel, len(arrays)),
        in_specs=[full] * len(arrays) + [pl.BlockSpec(memory_space=pl.ANY)] * len(after),
        out_specs=full,
        out_shape=jax.ShapeDtypeStruct((len(arrays),) + arrays[0].shape, arrays[0].dtype),
        name="pack_shards",
    )(*arrays, *after)


class Links:
    def __init__(self):
        self.dp_size = lax.axis_size("dp")
        self.hi_size = self.dp_size // 4
        index = lax.axis_index("dp")
        self.core = index & 1
        self.at = {"lo": (index >> 1) & 1, "tensor": lax.axis_index("tensor")}
        self.hi = index >> 2

    def over_dp(self, v, mask):
        return lax.ppermute(v, "dp", [(i, i ^ mask) for i in range(self.dp_size)])

    def swap(self, v, axis):
        if axis == "tensor":
            return lax.ppermute(v, "tensor", [(0, 1), (1, 0)])
        return self.over_dp(v, {"core": 1, "lo": 2}[axis])

    def over_hi(self, v, distance):
        return self.over_dp(v, 4 * distance)


def place_kernel(order, where, mine_ref, other_ref, *out_refs):
    hi_size = mine_ref.shape[2]

    def step(distance, carry):
        for i in range(2):
            for j in range(2):
                at = dict(zip(order, (where[0 if order[0] == "lo" else 1] ^ j, where[0 if order[1] == "lo" else 1] ^ i)))
                base = ((where[2] ^ distance) * 2 + at["lo"]) * 2
                for w, out_ref in enumerate(out_refs):
                    out_ref[at["tensor"], base + where[3]] = mine_ref[i, j, distance, w]
                    out_ref[at["tensor"], base + (1 - where[3])] = other_ref[i, j, distance, w]
        return carry

    lax.fori_loop(0, hi_size, step, 0)


def gather_tree(links, shards_in, order, after):
    stage = pack(shards_in, after[0])
    stage = pack([stage] + [links.over_hi(stage, d) for d in range(1, links.hi_size)], after[1])
    stage = jnp.stack([stage, links.swap(stage, order[0])])
    second = [stage, links.swap(stage, order[1])]
    stage = pack(second, after[2]) if after[2] else jnp.stack(second)
    other = links.swap(stage, "core")
    rows, columns = shards_in[0].shape
    where = jnp.stack([links.at["lo"], links.at["tensor"], links.hi, links.core]).astype(jnp.int32)
    blocks = links.dp_size
    full = pl.BlockSpec(memory_space=pltpu.VMEM)
    placed = pl.pallas_call(
        functools.partial(place_kernel, order),
        in_specs=[pl.BlockSpec(memory_space=pltpu.SMEM), full, full],
        out_specs=[full] * len(shards_in),
        out_shape=[jax.ShapeDtypeStruct((2, blocks, rows, columns), BF)] * len(shards_in),
        compiler_params=pltpu.CompilerParams(vmem_limit_bytes=48 * 1024 * 1024),
        cost_estimate=pl.CostEstimate(flops=0, bytes_accessed=4 * stage.size * 2, transcendentals=0),
        name="place_shards",
    )(where, stage, other)
    return [p.reshape(2, blocks * rows, columns) for p in placed]


def pick(v, index, axis=0):
    return lax.dynamic_index_in_dim(v, index, axis, keepdims=False)


def add_low(a, b):
    return (a.astype(F32) + b.astype(F32)).astype(BF)


def halve_cores(links, parts):
    blocks = [[g.reshape(links.hi_size, 2, 2, -1, g.shape[1]) for g in half] for half in parts]

    def side(core):
        return jnp.stack([jnp.stack([pick(g, core, 2) for g in half]) for half in blocks])

    return add_low(side(links.core), links.swap(side(1 - links.core), "core"))


def halve(links, total, axis, at):
    here = links.at[axis]
    return add_low(pick(total, here, at), links.swap(pick(total, 1 - here, at), axis))


def finish(links, total):
    out = pick(total, links.hi, 1).astype(F32)
    for d in range(1, links.hi_size):
        out = out + links.over_hi(pick(total, links.hi ^ d, 1), d).astype(F32)
    return [out[w] for w in range(out.shape[0])]


def sum_everywhere(links, vec):
    vec = vec + links.swap(vec, "tensor")
    bit = 1
    while bit < links.dp_size:
        vec = vec + links.over_dp(vec, bit)
        bit *= 2
    return vec


def split_vec(vec, sizes):
    out, at = [], 0
    for size in sizes:
        out.append(lax.slice_in_dim(vec, at, at + size))
        at += size
    return out


def shards(
    inputs,
    lengths,
    query_weight,
    key_weight,
    value_weight,
    query_bias,
    value_bias,
    out_weight,
    out_bias,
    first_gain,
    first_shift,
    input_projection_weight,
    input_projection_bias,
    output_projection_weight,
    output_projection_bias,
    second_gain,
    second_shift,
    out_cotangent,
):
    links = Links()
    half, seqs, _ = inputs.shape
    rows = half * seqs
    width = D // 2
    hidden_width = FF // 2
    tindex = jnp.reshape(links.at["tensor"], (1,)).astype(jnp.int32)
    everywhere = ("tensor", "dp")

    ffn_w = lax.all_gather(
        jnp.concatenate([input_projection_weight, output_projection_weight.T], 1), everywhere, axis=0, tiled=True
    ).reshape(2, D, 2 * hidden_width)
    up_w = [ffn_w[t, :, :hidden_width] for t in range(2)]
    down_w = [ffn_w[t, :, hidden_width:] for t in range(2)]
    inputs_seq = inputs.transpose(1, 0, 2).reshape(rows, D)
    rows_low = inputs_seq.astype(BF)
    rows_other = links.swap(rows_low, "tensor")
    cotangent = out_cotangent.transpose(1, 0, 2).reshape(rows, D)
    second_shift_part = jnp.sum(cotangent, axis=0)
    scaled_mean = jnp.mean(cotangent * second_gain, -1, keepdims=True)
    idle = [cotangent, second_shift_part, scaled_mean.reshape(seqs, half)]
    query_w, key_w = gather_tree(
        links, [query_weight, key_weight], ("tensor", "lo"), [[rows_low], [rows_other], idle]
    )
    value_w, out_w = gather_tree(links, [value_weight, out_weight.T], ("lo", "tensor"), [[rows_low], [], []])
    queries, keys, values = project(rows_low, rows_other, query_w, key_w, value_w, query_bias, value_bias, seqs)
    context, log_sums = [], []
    for t in range(2):
        ctx, lse = attend_forward(lengths, tindex, queries[t], keys[t], values[t], seqs)
        context.append(ctx)
        log_sums.append(lse)
    attention = dot(context[0], out_w[0], 1, 1) + dot(context[1], out_w[1], 1, 1)
    hidden, normed_one, inv_one = layer_norm(inputs_seq + attention + out_bias, first_gain, first_shift)
    hidden_low = hidden.astype(BF)
    acts, slopes = [], []
    for t in range(2):
        pre = dot(hidden_low, up_w[t], 1, 0) + input_projection_bias[t * hidden_width : (t + 1) * hidden_width]
        act, slope = gelu_both(pre)
        acts.append(act.astype(BF))
        slopes.append(lax.optimization_barrier(slope.astype(BF)))
    branch = dot(acts[0], down_w[0], 1, 1) + dot(acts[1], down_w[1], 1, 1)
    outputs, normed_two, inv_two = layer_norm(
        hidden + branch + output_projection_bias, second_gain, second_shift
    )
    second_grad = norm_back(cotangent, normed_two, inv_two, second_gain)
    second_gain_part = jnp.sum(cotangent * normed_two, axis=0)
    down_bias_part = jnp.sum(second_grad, axis=0)
    second_low = second_grad.astype(BF)
    down_chip = halve_cores(links, [[dot(second_low, acts[t], 0, 0).astype(BF)] for t in range(2)])
    pre_grads, up_bias_parts = [], []
    for t in range(2):
        pre_grad = (dot(second_low, down_w[t], 1, 0) * slopes[t].astype(F32)).astype(BF)
        pre_grads.append(pre_grad)
        up_bias_parts.append(jnp.sum(pre_grad, axis=0, dtype=F32))
    up_chip = halve_cores(links, [[dot(hidden_low, pre_grads[t], 0, 0).astype(BF)] for t in range(2)])
    hidden_grad = second_grad + (dot(pre_grads[0], up_w[0], 1, 1) + dot(pre_grads[1], up_w[1], 1, 1))
    first_grad = norm_back(hidden_grad, normed_one, inv_one, first_gain)
    first_gain_part = jnp.sum(hidden_grad * normed_one, axis=0)
    first_shift_part = jnp.sum(hidden_grad, axis=0)
    out_bias_part = jnp.sum(first_grad, axis=0)
    first_low = first_grad.astype(BF)
    down_half = halve(links, down_chip, "tensor", 0)
    up_half = halve(links, up_chip, "lo", 3)
    query_grads, key_grads, value_grads, bias_parts, chip = [], [], [], [], []
    down_quarter = halve(links, down_half, "lo", 2)
    up_quarter = halve(links, up_half, "tensor", 0)
    after = [down_chip, up_chip]
    for t in range(2):
        context_grad = dot(first_low, out_w[t], 1, 0).astype(BF)
        dq, dk, dv, sums = attend_backward(
            lengths, tindex, queries[t], keys[t], values[t], context[t], log_sums[t], context_grad, seqs, after
        )
        query_grads.append(dq)
        key_grads.append(dk)
        value_grads.append(dv)
        bias_parts.append(sums)
        if t == 1:
            other_total = back_product(
                [(key_grads[i], 1, key_w, i) for i in range(2)] + [(value_grads[i], 1, value_w, i) for i in range(2)],
                None,
                BF,
                seqs,
                [chip[0]],
            )
            after = [other_total, down_quarter, up_quarter]
        total, made = weight_products(
            links, rows_low, rows_other, first_low, dq, dk, dv, context[t], after if t else []
        )
        chip.append(total)
        after = [down_half, up_half, made, total]
    from_other = links.swap(other_total, "tensor")
    chip_half = [halve(links, c, "lo", 2) for c in chip]
    vectors = jnp.concatenate(
            [
                out_bias_part,
                first_gain_part,
                first_shift_part,
                down_bias_part,
                second_gain_part,
                second_shift_part,
                *up_bias_parts,
                bias_parts[0][0],
                bias_parts[1][0],
                bias_parts[0][1],
                bias_parts[1][1],
            ]
        ).reshape(-1, 128)
    sums = sum_everywhere(links, pack([vectors], [chip[1], chip_half[0]])[0]).reshape(-1)
    (
        out_bias_sum,
        first_gain_sum,
        first_shift_sum,
        down_bias_sum,
        second_gain_sum,
        second_shift_sum,
        up_bias_sum,
        query_bias_sum,
        value_bias_sum,
    ) = split_vec(sums, [D] * 6 + [FF, D, D])
    own_total = back_product(
        [(query_grads[t], None, query_w, t) for t in range(2)]
        + [(key_grads[t], 0, key_w, t) for t in range(2)]
        + [(value_grads[t], 0, value_w, t) for t in range(2)],
        first_grad,
        F32,
        seqs,
        [],
    )
    input_grad = own_total + from_other.astype(F32)
    (down_sum,) = finish(links, down_quarter)
    (up_sum,) = finish(links, up_quarter)
    first_side = links.at["tensor"] == 0
    mine = jnp.where(first_side, chip_half[0], chip_half[1])
    theirs = jnp.where(first_side, chip_half[1], chip_half[0])
    query_sum, key_sum, value_sum, out_sum = finish(
        links, add_low(mine, links.swap(pack([theirs], [from_other])[0], "tensor"))
    )

    def positions_first(v):
        return v.reshape(seqs, half, D).transpose(1, 0, 2)

    return (
        positions_first(outputs),
        positions_first(input_grad),
        query_sum,
        key_sum,
        value_sum,
        query_bias_sum,
        value_bias_sum,
        out_sum.T,
        out_bias_sum,
        first_gain_sum,
        first_shift_sum,
        up_sum,
        up_bias_sum,
        down_sum.T,
        down_bias_sum,
        second_gain_sum,
        second_shift_sum,
    )


def solution(mesh):
    in_specs = (
        P("tensor", "dp", None),
        P("dp"),
        P("dp", "tensor"),
        P("dp", "tensor"),
        P("dp", "tensor"),
        P(),
        P(),
        P("tensor", "dp"),
        P(),
        P(),
        P(),
        P("dp", "tensor"),
        P(),
        P("tensor", "dp"),
        P(),
        P(),
        P(),
        P("tensor", "dp", None),
    )
    out_specs = (
        P("tensor", "dp", None),
        P("tensor", "dp", None),
        P("dp", "tensor"),
        P("dp", "tensor"),
        P("dp", "tensor"),
        P(),
        P(),
        P("tensor", "dp"),
        P(),
        P(),
        P(),
        P("dp", "tensor"),
        P(),
        P("tensor", "dp"),
        P(),
        P(),
        P(),
    )
    return jax.shard_map(shards, mesh=mesh, in_specs=in_specs, out_specs=out_specs, check_vma=False)
```

```python
import functools

import jax
import jax.numpy as jnp
from jax import lax
from jax.experimental import pallas as pl
from jax.experimental.pallas import tpu as pltpu
from jax.sharding import PartitionSpec as P

D = 768
H = 12
HD = 64
FF = 3072

NORM_EPSILON = 1e-12
BF = jnp.bfloat16
F32 = jnp.float32


def dot(a, b, da, db):
    return lax.dot_general(a, b, (((da,), (db,)), ((), ())), preferred_element_type=F32)


def layer_norm(resid, gain_vec, shift_vec):
    mean_value = jnp.mean(resid, -1, keepdims=True)
    centred = resid - mean_value
    variance = jnp.mean(centred * centred, -1, keepdims=True)
    inv_std = lax.rsqrt(variance + NORM_EPSILON)
    normed = centred * inv_std
    return (normed * gain_vec + shift_vec, normed, inv_std)


def norm_back(grad_in, normed, inv_std, gain_vec):
    scaled = grad_in * gain_vec
    return inv_std * (
        scaled
        - jnp.mean(scaled, -1, keepdims=True)
        - normed * jnp.mean(scaled * normed, -1, keepdims=True)
    )


def gelu_both(v):
    z = jnp.abs(v) * (0.5**0.5)
    t = 1.0 / (1.0 + 0.3275911 * z)
    gauss = jnp.exp(-0.5 * v * v)
    poly = t * (
        0.5 * 0.254829592
        + t * (0.5 * -0.284496736 + t * (0.5 * 1.421413741 + t * (0.5 * -1.453152027 + t * (0.5 * 1.061405429))))
    )
    tail = poly * gauss
    phi_cum = jnp.where(v < 0, tail, 1.0 - tail)
    return v * phi_cum, phi_cum + v * gauss * 0.3989422804014327


def mask_bias(half, axis, length, place):
    shape = (1, half) if axis else (half, 1)
    at = lax.broadcasted_iota(jnp.int32, shape, axis)
    parts = [jnp.where(at + p * half < length, 0.0, -1e30) for p in (place, 1 - place)]
    return jnp.concatenate(parts, axis)


def attend_forward_kernel(heads, half, lens, tindex, q_ref, k_ref, v_ref, ctx_ref, lse_ref):
    bias = mask_bias(half, 1, lens[pl.program_id(0)], tindex[0])
    col = lax.broadcasted_iota(jnp.int32, (half, 128), 1)
    lse_tile = jnp.zeros((half, 128), F32)
    for h in range(heads):
        sl = slice(h * HD, (h + 1) * HD)
        k = k_ref[:, :, sl].reshape(2 * half, HD)
        v = v_ref[:, :, sl].reshape(2 * half, HD)
        s = dot(q_ref[:, sl], k, 1, 1) + bias
        m = jnp.max(s, -1, keepdims=True)
        e = jnp.exp(s - m)
        total = jnp.sum(e, -1, keepdims=True)
        ctx_ref[:, sl] = (dot(e.astype(BF), v, 1, 0) / total).astype(BF)
        lse_tile = jnp.where(col == h, m + jnp.log(total), lse_tile)
    lse_ref[0] = lse_tile


def attend_backward_kernel(
    heads, half, lens, tindex, q_ref, k_ref, v_ref, ctx_ref, lse_ref, dctx_ref, *rest
):
    dq_ref, dk_ref, dv_ref, sums_ref = rest[-4:]
    bias = mask_bias(half, 0, lens[pl.program_id(0)], tindex[0])
    lse_rows = jnp.transpose(lse_ref[0])
    prod = ctx_ref[...].astype(F32) * dctx_ref[...].astype(F32)
    col = lax.broadcasted_iota(jnp.int32, (half, 128), 1)
    delta_tile = jnp.zeros((half, 128), F32)
    for h in range(heads):
        delta_tile = jnp.where(
            col == h, jnp.sum(prod[:, h * HD : (h + 1) * HD], -1, keepdims=True), delta_tile
        )
    delta_rows = jnp.transpose(delta_tile)
    for h in range(heads):
        sl = slice(h * HD, (h + 1) * HD)
        q = q_ref[:, sl]
        dc = dctx_ref[:, sl]
        k = k_ref[:, :, sl].reshape(2 * half, HD)
        v = v_ref[:, :, sl].reshape(2 * half, HD)
        p = jnp.exp(dot(k, q, 1, 1) + bias - lse_rows[h : h + 1, :])
        ds = (p * (dot(v, dc, 1, 1) - delta_rows[h : h + 1, :])).astype(BF)
        dk_ref[:, :, sl] = dot(ds, q, 1, 0).astype(BF).reshape(2, half, HD)
        dv = dot(p.astype(BF), dc, 1, 0).astype(BF)
        dv_ref[:, :, sl] = dv.reshape(2, half, HD)
        dq = (dot(ds, k, 0, 0) * HD**-0.5).astype(BF)
        dq_ref[:, sl] = dq
        sums_ref[0, 0:1, sl] = jnp.sum(dq.astype(F32), 0, keepdims=True)
        sums_ref[0, 1:2, sl] = jnp.sum(dv.astype(F32), 0, keepdims=True)


def attend_specs(half, width):
    rows = pl.BlockSpec((half, width), lambda s, *_: (s, 0))
    pair = pl.BlockSpec((2, half, width), lambda s, *_: (0, s, 0))
    stat = pl.BlockSpec((1, half, 128), lambda s, *_: (s, 0, 0))
    return rows, pair, stat


def attend_forward(lengths, tindex, q, k, v, seqs):
    rows, width = q.shape
    half = rows // seqs
    flat, pair, stat = attend_specs(half, width)
    return pl.pallas_call(
        functools.partial(attend_forward_kernel, width // HD, half),
        grid_spec=pltpu.PrefetchScalarGridSpec(
            num_scalar_prefetch=2, grid=(seqs,), in_specs=[flat, pair, pair], out_specs=[flat, stat]
        ),
        out_shape=[
            jax.ShapeDtypeStruct((rows, width), BF),
            jax.ShapeDtypeStruct((seqs, half, 128), F32),
        ],
        compiler_params=pltpu.CompilerParams(vmem_limit_bytes=24 * 1024 * 1024),
        cost_estimate=pl.CostEstimate(flops=8_000_000_000, bytes_accessed=5_000_000, transcendentals=3_500_000),
        name="attend_forward",
    )(lengths, tindex, q, k, v)


def attend_backward(lengths, tindex, q, k, v, ctx, lse, dctx, seqs, after):
    rows, width = q.shape
    half = rows // seqs
    flat, pair, stat = attend_specs(half, width)
    dq, dk, dv, sums = pl.pallas_call(
        functools.partial(attend_backward_kernel, width // HD, half),
        grid_spec=pltpu.PrefetchScalarGridSpec(
            num_scalar_prefetch=2,
            grid=(seqs,),
            in_specs=[flat, pair, pair, flat, stat, flat] + [pl.BlockSpec(memory_space=pl.ANY)] * len(after),
            out_specs=[flat, pair, pair, pl.BlockSpec((1, 2, width), lambda s, *_: (s, 0, 0))],
        ),
        out_shape=[
            jax.ShapeDtypeStruct((rows, width), BF),
            jax.ShapeDtypeStruct((2, rows, width), BF),
            jax.ShapeDtypeStruct((2, rows, width), BF),
            jax.ShapeDtypeStruct((seqs, 2, width), F32),
        ],
        compiler_params=pltpu.CompilerParams(vmem_limit_bytes=24 * 1024 * 1024),
        cost_estimate=pl.CostEstimate(flops=18_000_000_000, bytes_accessed=10_000_000, transcendentals=3_500_000),
        name="attend_backward",
    )(lengths, tindex, q, k, v, ctx, lse, dctx, *after)
    return dq, dk, dv, jnp.sum(sums, 0)


def back_kernel(count, has_base, *refs):
    out_ref = refs[-1]
    total = refs[2 * count][...] if has_base else None
    for i in range(count):
        g = refs[i][...].reshape(out_ref.shape[0], -1)
        part = dot(g, refs[count + i][0], 1, 1)
        total = part if total is None else total + part
    out_ref[...] = total.astype(out_ref.dtype)


def back_product(terms, base, dtype, seqs, after):
    block = (base if base is not None else terms[0][0]).shape[-2] // seqs
    specs, weight_specs = [], []
    for grad, side, weight, t in terms:
        if side is None:
            specs.append(pl.BlockSpec((block, grad.shape[1]), lambda i: (i, 0)))
        else:
            specs.append(pl.BlockSpec((1, block, grad.shape[2]), lambda i, side=side: (side, i, 0)))
        weight_specs.append(pl.BlockSpec((1,) + weight.shape[1:], lambda i, t=t: (t, 0, 0)))
    out_spec = pl.BlockSpec((block, D), lambda i: (i, 0))
    args = [x[0] for x in terms] + [x[2] for x in terms] + ([base] if base is not None else [])
    return pl.pallas_call(
        functools.partial(back_kernel, len(terms), base is not None),
        grid=(seqs,),
        in_specs=specs
        + weight_specs
        + ([out_spec] if base is not None else [])
        + [pl.BlockSpec(memory_space=pl.ANY)] * len(after),
        out_specs=out_spec,
        out_shape=jax.ShapeDtypeStruct((block * seqs, D), dtype),
        compiler_params=pltpu.CompilerParams(vmem_limit_bytes=32 * 1024 * 1024),
        cost_estimate=pl.CostEstimate(
            flops=sum(2 * block * seqs * w.shape[1] * w.shape[2] for _, _, w, _ in terms),
            bytes_accessed=8_000_000,
            transcendentals=0,
        ),
        name="back_product",
    )(*args, *after)


def weight_kernel(core, own_ref, oth_ref, first_ref, dq_ref, dk_ref, dv_ref, ctx_ref, *rest):
    keep_ref, send_ref = rest[-2:]
    _, blocks, rows, columns = keep_ref.shape
    own = jnp.transpose(own_ref[...])
    oth = jnp.transpose(oth_ref[...])
    first = core[0] == 0

    def put(w, full):
        full = full.astype(BF).reshape(blocks, 2, rows, columns)
        keep_ref[w] = jnp.where(first, full[:, 0], full[:, 1])
        send_ref[w] = jnp.where(first, full[:, 1], full[:, 0])

    put(0, dot(own, dq_ref[...], 1, 0))
    put(1, dot(own, dk_ref[0], 1, 0) + dot(oth, dk_ref[1], 1, 0))
    put(2, dot(own, dv_ref[0], 1, 0) + dot(oth, dv_ref[1], 1, 0))
    put(3, dot(jnp.transpose(first_ref[...]), ctx_ref[...], 1, 0))


def weight_products(links, own, oth, first_low, dq, dk, dv, ctx, after):
    rows = D // links.dp_size
    columns = dq.shape[-1]
    if rows % 16:
        both = jnp.concatenate([own, oth], 0)
        parts = [
            dot(own, dq, 0, 0),
            dot(both, dk.reshape(-1, columns), 0, 0),
            dot(both, dv.reshape(-1, columns), 0, 0),
            dot(first_low, ctx, 0, 0),
        ]
        return halve_cores(links, [[p.astype(BF) for p in parts]])[0], parts[0]
    shape = (4, links.dp_size // 2, rows, columns)
    full = pl.BlockSpec(memory_space=pltpu.VMEM)
    keep, send = pl.pallas_call(
        weight_kernel,
        in_specs=[pl.BlockSpec(memory_space=pltpu.SMEM)]
        + [full] * 7
        + [pl.BlockSpec(memory_space=pl.ANY)] * len(after),
        out_specs=[full, full],
        out_shape=[jax.ShapeDtypeStruct(shape, BF)] * 2,
        compiler_params=pltpu.CompilerParams(vmem_limit_bytes=40 * 1024 * 1024),
        cost_estimate=pl.CostEstimate(
            flops=2 * D * columns * own.shape[0] * 6, bytes_accessed=10_000_000, transcendentals=0
        ),
        name="weight_products",
    )(links.core.reshape(1).astype(jnp.int32), own, oth, first_low, dq, dk, dv, ctx, *after)
    total = add_low(keep, links.swap(send, "core"))
    return total.reshape(4, links.hi_size, 2, rows, columns), keep


def project_kernel(
    own_ref, oth_ref, qw_ref, kw_ref, vw_ref, qb_ref, vb_ref, q0, q1, k0, k1, v0, v1
):
    own, oth = own_ref[...], oth_ref[...]
    for t, (q, k, v) in enumerate(((q0, k0, v0), (q1, k1, v1))):
        q[...] = ((dot(own, qw_ref[t], 1, 0) + qb_ref[t]).astype(BF) * jnp.array(HD**-0.5, BF)).astype(BF)
        for i, x in enumerate((own, oth)):
            k[i] = dot(x, kw_ref[t], 1, 0).astype(BF)
            v[i] = (dot(x, vw_ref[t], 1, 0) + vb_ref[t]).astype(BF)


def project(own, oth, query_w, key_w, value_w, query_bias, value_bias, seqs):
    rows, width = own.shape[0], query_w.shape[2]
    half = rows // seqs
    full = pl.BlockSpec(memory_space=pltpu.VMEM)
    flat = pl.BlockSpec((half, width), lambda i: (i, 0))
    pair = pl.BlockSpec((2, half, width), lambda i: (0, i, 0))
    q0, q1, k0, k1, v0, v1 = pl.pallas_call(
        project_kernel,
        grid=(seqs,),
        in_specs=[pl.BlockSpec((half, D), lambda i: (i, 0))] * 2 + [full] * 5,
        out_specs=[flat, flat, pair, pair, pair, pair],
        out_shape=[jax.ShapeDtypeStruct((rows, width), BF)] * 2 + [jax.ShapeDtypeStruct((2, rows, width), BF)] * 4,
        compiler_params=pltpu.CompilerParams(vmem_limit_bytes=32 * 1024 * 1024),
        cost_estimate=pl.CostEstimate(flops=2 * 10 * rows * D * width, bytes_accessed=16_000_000, transcendentals=0),
        name="project",
    )(
        own,
        oth,
        query_w,
        key_w,
        value_w,
        query_bias.reshape(2, 1, width),
        value_bias.reshape(2, 1, width),
    )
    return [q0, q1], [k0, k1], [v0, v1]


def pack_kernel(count, *refs):
    for i in range(count):
        refs[-1][i] = refs[i][...]


def pack(arrays, after):
    full = pl.BlockSpec(memory_space=pltpu.VMEM)
    return pl.pallas_call(
        functools.partial(pack_kernel, len(arrays)),
        in_specs=[full] * len(arrays) + [pl.BlockSpec(memory_space=pl.ANY)] * len(after),
        out_specs=full,
        out_shape=jax.ShapeDtypeStruct((len(arrays),) + arrays[0].shape, arrays[0].dtype),
        name="pack_shards",
    )(*arrays, *after)


class Links:
    def __init__(self):
        self.dp_size = lax.axis_size("dp")
        self.hi_size = self.dp_size // 4
        index = lax.axis_index("dp")
        self.core = index & 1
        self.at = {"lo": (index >> 1) & 1, "tensor": lax.axis_index("tensor")}
        self.hi = index >> 2

    def over_dp(self, v, mask):
        return lax.ppermute(v, "dp", [(i, i ^ mask) for i in range(self.dp_size)])

    def swap(self, v, axis):
        if axis == "tensor":
            return lax.ppermute(v, "tensor", [(0, 1), (1, 0)])
        return self.over_dp(v, {"core": 1, "lo": 2}[axis])

    def over_hi(self, v, distance):
        return self.over_dp(v, 4 * distance)


def place_kernel(order, where, mine_ref, other_ref, *out_refs):
    hi_size = mine_ref.shape[2]

    def step(distance, carry):
        for i in range(2):
            for j in range(2):
                at = dict(zip(order, (where[0 if order[0] == "lo" else 1] ^ j, where[0 if order[1] == "lo" else 1] ^ i)))
                base = ((where[2] ^ distance) * 2 + at["lo"]) * 2
                for w, out_ref in enumerate(out_refs):
                    out_ref[at["tensor"], base + where[3]] = mine_ref[i, j, distance, w]
                    out_ref[at["tensor"], base + (1 - where[3])] = other_ref[i, j, distance, w]
        return carry

    lax.fori_loop(0, hi_size, step, 0)


def gather_tree(links, shards_in, order, after):
    stage = pack(shards_in, after[0])
    stage = pack([stage] + [links.over_hi(stage, d) for d in range(1, links.hi_size)], after[1])
    stage = jnp.stack([stage, links.swap(stage, order[0])])
    second = [stage, links.swap(stage, order[1])]
    stage = pack(second, after[2]) if after[2] else jnp.stack(second)
    other = links.swap(stage, "core")
    rows, columns = shards_in[0].shape
    where = jnp.stack([links.at["lo"], links.at["tensor"], links.hi, links.core]).astype(jnp.int32)
    blocks = links.dp_size
    full = pl.BlockSpec(memory_space=pltpu.VMEM)
    placed = pl.pallas_call(
        functools.partial(place_kernel, order),
        in_specs=[pl.BlockSpec(memory_space=pltpu.SMEM), full, full],
        out_specs=[full] * len(shards_in),
        out_shape=[jax.ShapeDtypeStruct((2, blocks, rows, columns), BF)] * len(shards_in),
        compiler_params=pltpu.CompilerParams(vmem_limit_bytes=48 * 1024 * 1024),
        cost_estimate=pl.CostEstimate(flops=0, bytes_accessed=4 * stage.size * 2, transcendentals=0),
        name="place_shards",
    )(where, stage, other)
    return [p.reshape(2, blocks * rows, columns) for p in placed]


def pick(v, index, axis=0):
    return lax.dynamic_index_in_dim(v, index, axis, keepdims=False)


def add_low(a, b):
    return (a.astype(F32) + b.astype(F32)).astype(BF)


def halve_cores(links, parts):
    blocks = [[g.reshape(links.hi_size, 2, 2, -1, g.shape[1]) for g in half] for half in parts]

    def side(core):
        return jnp.stack([jnp.stack([pick(g, core, 2) for g in half]) for half in blocks])

    return add_low(side(links.core), links.swap(side(1 - links.core), "core"))


def halve(links, total, axis, at):
    here = links.at[axis]
    return add_low(pick(total, here, at), links.swap(pick(total, 1 - here, at), axis))


def finish(links, total):
    out = pick(total, links.hi, 1).astype(F32)
    for d in range(1, links.hi_size):
        out = out + links.over_hi(pick(total, links.hi ^ d, 1), d).astype(F32)
    return [out[w] for w in range(out.shape[0])]


def sum_everywhere(links, vec):
    vec = vec + links.swap(vec, "tensor")
    bit = 1
    while bit < links.dp_size:
        vec = vec + links.over_dp(vec, bit)
        bit *= 2
    return vec


def split_vec(vec, sizes):
    out, at = [], 0
    for size in sizes:
        out.append(lax.slice_in_dim(vec, at, at + size))
        at += size
    return out


def shards(
    inputs,
    lengths,
    query_weight,
    key_weight,
    value_weight,
    query_bias,
    value_bias,
    out_weight,
    out_bias,
    first_gain,
    first_shift,
    input_projection_weight,
    input_projection_bias,
    output_projection_weight,
    output_projection_bias,
    second_gain,
    second_shift,
    out_cotangent,
):
    links = Links()
    half, seqs, _ = inputs.shape
    rows = half * seqs
    width = D // 2
    hidden_width = FF // 2
    tindex = jnp.reshape(links.at["tensor"], (1,)).astype(jnp.int32)
    everywhere = ("tensor", "dp")

    ffn_w = lax.all_gather(
        jnp.concatenate([input_projection_weight, output_projection_weight.T], 1), everywhere, axis=0, tiled=True
    ).reshape(2, D, 2 * hidden_width)
    up_w = [ffn_w[t, :, :hidden_width] for t in range(2)]
    down_w = [ffn_w[t, :, hidden_width:] for t in range(2)]
    inputs_seq = inputs.transpose(1, 0, 2).reshape(rows, D)
    rows_low = inputs_seq.astype(BF)
    rows_other = links.swap(rows_low, "tensor")
    cotangent = out_cotangent.transpose(1, 0, 2).reshape(rows, D)
    second_shift_part = jnp.sum(cotangent, axis=0)
    scaled_mean = jnp.mean(cotangent * second_gain, -1, keepdims=True)
    idle = [cotangent, second_shift_part, scaled_mean.reshape(seqs, half)]
    query_w, key_w = gather_tree(
        links, [query_weight, key_weight], ("tensor", "lo"), [[rows_low], [rows_other], idle]
    )
    value_w, out_w = gather_tree(links, [value_weight, out_weight.T], ("lo", "tensor"), [[rows_low], [], []])
    queries, keys, values = project(rows_low, rows_other, query_w, key_w, value_w, query_bias, value_bias, seqs)
    context, log_sums = [], []
    for t in range(2):
        ctx, lse = attend_forward(lengths, tindex, queries[t], keys[t], values[t], seqs)
        context.append(ctx)
        log_sums.append(lse)
    attention = dot(context[0], out_w[0], 1, 1) + dot(context[1], out_w[1], 1, 1)
    hidden, normed_one, inv_one = layer_norm(inputs_seq + attention + out_bias, first_gain, first_shift)
    hidden_low = hidden.astype(BF)
    acts, slopes = [], []
    for t in range(2):
        pre = dot(hidden_low, up_w[t], 1, 0) + input_projection_bias[t * hidden_width : (t + 1) * hidden_width]
        act, slope = gelu_both(pre)
        acts.append(act.astype(BF))
        slopes.append(lax.optimization_barrier(slope.astype(BF)))
    branch = dot(acts[0], down_w[0], 1, 1) + dot(acts[1], down_w[1], 1, 1)
    outputs, normed_two, inv_two = layer_norm(
        hidden + branch + output_projection_bias, second_gain, second_shift
    )
    second_grad = norm_back(cotangent, normed_two, inv_two, second_gain)
    second_gain_part = jnp.sum(cotangent * normed_two, axis=0)
    down_bias_part = jnp.sum(second_grad, axis=0)
    second_low = second_grad.astype(BF)
    down_chip = halve_cores(links, [[dot(second_low, acts[t], 0, 0).astype(BF)] for t in range(2)])
    pre_grads, up_bias_parts = [], []
    for t in range(2):
        pre_grad = (dot(second_low, down_w[t], 1, 0) * slopes[t].astype(F32)).astype(BF)
        pre_grads.append(pre_grad)
        up_bias_parts.append(jnp.sum(pre_grad, axis=0, dtype=F32))
    up_chip = halve_cores(links, [[dot(hidden_low, pre_grads[t], 0, 0).astype(BF)] for t in range(2)])
    hidden_grad = second_grad + (dot(pre_grads[0], up_w[0], 1, 1) + dot(pre_grads[1], up_w[1], 1, 1))
    first_grad = norm_back(hidden_grad, normed_one, inv_one, first_gain)
    first_gain_part = jnp.sum(hidden_grad * normed_one, axis=0)
    first_shift_part = jnp.sum(hidden_grad, axis=0)
    out_bias_part = jnp.sum(first_grad, axis=0)
    first_low = first_grad.astype(BF)
    down_half = halve(links, down_chip, "tensor", 0)
    up_half = halve(links, up_chip, "lo", 3)
    query_grads, key_grads, value_grads, bias_parts, chip = [], [], [], [], []
    down_quarter = halve(links, down_half, "lo", 2)
    up_quarter = halve(links, up_half, "tensor", 0)
    after = [down_chip, up_chip]
    for t in range(2):
        context_grad = dot(first_low, out_w[t], 1, 0).astype(BF)
        dq, dk, dv, sums = attend_backward(
            lengths, tindex, queries[t], keys[t], values[t], context[t], log_sums[t], context_grad, seqs, after
        )
        query_grads.append(dq)
        key_grads.append(dk)
        value_grads.append(dv)
        bias_parts.append(sums)
        if t == 1:
            other_total = back_product(
                [(key_grads[i], 1, key_w, i) for i in range(2)] + [(value_grads[i], 1, value_w, i) for i in range(2)],
                None,
                BF,
                seqs,
                [chip[0]],
            )
            after = [other_total, down_quarter, up_quarter]
        total, made = weight_products(
            links, rows_low, rows_other, first_low, dq, dk, dv, context[t], after if t else []
        )
        chip.append(total)
        after = [down_half, up_half, made, total]
    from_other = links.swap(other_total, "tensor")
    chip_half = [halve(links, c, "lo", 2) for c in chip]
    vectors = jnp.concatenate(
            [
                out_bias_part,
                first_gain_part,
                first_shift_part,
                down_bias_part,
                second_gain_part,
                second_shift_part,
                *up_bias_parts,
                bias_parts[0][0],
                bias_parts[1][0],
                bias_parts[0][1],
                bias_parts[1][1],
            ]
        ).reshape(-1, 128)
    first_side = links.at["tensor"] == 0
    mine = jnp.where(first_side, chip_half[0], chip_half[1])
    theirs = jnp.where(first_side, chip_half[1], chip_half[0])
    total_half = add_low(mine, links.swap(theirs, "tensor"))
    sums = sum_everywhere(links, pack([vectors], [total_half])[0]).reshape(-1)
    (
        out_bias_sum,
        first_gain_sum,
        first_shift_sum,
        down_bias_sum,
        second_gain_sum,
        second_shift_sum,
        up_bias_sum,
        query_bias_sum,
        value_bias_sum,
    ) = split_vec(sums, [D] * 6 + [FF, D, D])
    own_total = back_product(
        [(query_grads[t], None, query_w, t) for t in range(2)]
        + [(key_grads[t], 0, key_w, t) for t in range(2)]
        + [(value_grads[t], 0, value_w, t) for t in range(2)],
        first_grad,
        F32,
        seqs,
        [],
    )
    input_grad = own_total + from_other.astype(F32)
    (down_sum,) = finish(links, down_quarter)
    (up_sum,) = finish(links, up_quarter)
    query_sum, key_sum, value_sum, out_sum = finish(links, total_half)

    def positions_first(v):
        return v.reshape(seqs, half, D).transpose(1, 0, 2)

    return (
        positions_first(outputs),
        positions_first(input_grad),
        query_sum,
        key_sum,
        value_sum,
        query_bias_sum,
        value_bias_sum,
        out_sum.T,
        out_bias_sum,
        first_gain_sum,
        first_shift_sum,
        up_sum,
        up_bias_sum,
        down_sum.T,
        down_bias_sum,
        second_gain_sum,
        second_shift_sum,
    )


def solution(mesh):
    in_specs = (
        P("tensor", "dp", None),
        P("dp"),
        P("dp", "tensor"),
        P("dp", "tensor"),
        P("dp", "tensor"),
        P(),
        P(),
        P("tensor", "dp"),
        P(),
        P(),
        P(),
        P("dp", "tensor"),
        P(),
        P("tensor", "dp"),
        P(),
        P(),
        P(),
        P("tensor", "dp", None),
    )
    out_specs = (
        P("tensor", "dp", None),
        P("tensor", "dp", None),
        P("dp", "tensor"),
        P("dp", "tensor"),
        P("dp", "tensor"),
        P(),
        P(),
        P("tensor", "dp"),
        P(),
        P(),
        P(),
        P("dp", "tensor"),
        P(),
        P("tensor", "dp"),
        P(),
        P(),
        P(),
    )
    return jax.shard_map(shards, mesh=mesh, in_specs=in_specs, out_specs=out_specs, check_vma=False)
```
